32 devices in a mesh: param: 8 (over z, x), ex: 4 (over y, core).
Axes of the slice: x: 2, y: 2, z: 4, core: 2. Of those that a mesh axis runs over, the one named last changes fastest.
Arguments:
- gradients: bfloat16 [512, 65536], P('ex', 'param'), may hold values from -60 to 60
- projection_seed: int32 [1], replicated, may hold values from 0 to 1048575
- target_features: bfloat16 [512, 4096], replicated, may hold values from -0.09375 to 0.09375
Outputs:
- scores: float32 [512, 512], P('param', 'ex')
The draws below stay inside these ranges and needn't reach their ends.
All inputs are finite; a program needn't handle non-finite values.
Results may differ from the reference program's by a relative error of at most 0.011.
Values may be sent and summed in bfloat16 or wider, within the bound.
A program may use at most 64 MiB of HBM per device.

```python
import math
import jax
import jax.numpy as jnp
from jax import lax

FEATS = 4096
BLOCK = 128
STEPS = 10
COORD_DEV = 8192
TARGET_ROWS = 512
COORDS = 65536
EXAMPLES = 512
N_PARAM = 8


def draw_gradients(key, part):
    key_noise, key_rows, key_cols = jax.random.split(key, 3)
    noise = jax.random.truncated_normal(key_noise, -5.0, 5.0, (EXAMPLES, COORDS), jnp.float32)
    col_scale = jnp.exp(jax.random.uniform(key_cols, (1, COORDS), jnp.float32, jnp.log(0.5), jnp.log(2.0)))
    row_scale = jnp.exp(jax.random.uniform(key_rows, (EXAMPLES, 1), jnp.float32, jnp.log(0.3), jnp.log(3.0)))
    return (noise * row_scale * col_scale).astype(jnp.bfloat16)


def gaussian(own_key, extent, spread, most, kind=jnp.bfloat16):
    return jnp.clip(spread * jax.random.normal(own_key, extent, jnp.float32), -most, most).astype(kind)


def setup_inputs(seed: int = 0) -> dict:
    arg_keys = jax.random.split(jax.random.key(seed), 4)
    return {
        "gradients": draw_gradients(jax.random.fold_in(arg_keys[3], 71), 0),
        "projection_seed": jax.random.randint(arg_keys[1], (1,), 0, 1048576).astype(jnp.int32),
        "target_features": gaussian(arg_keys[2], (TARGET_ROWS, FEATS), FEATS ** -0.5, 0.09375),
    }


DAMPING = 0.001

def hashed(seed_value, row_start, row_count, col_start, col_count, total_coords):
    row_index = (row_start + lax.iota(jnp.int32, row_count)).reshape(row_count, 1)
    col_index = (col_start + lax.iota(jnp.int32, col_count)).reshape(1, col_count)
    mixed = row_index * 73856093 ^ col_index * 19349663 ^ seed_value * 83492791
    mixed = mixed ^ jnp.right_shift(mixed, 13)
    mixed = mixed * 1274126177
    mixed = mixed ^ jnp.right_shift(mixed, 16)
    uniform_value = (mixed & 65535).astype(jnp.float32) * (1.0 / 65536.0)
    return ((2.0 * uniform_value - 1.0) * math.sqrt(3.0 / total_coords)).astype(jnp.bfloat16)

def newton_inverse(fisher):
    width = fisher.shape[1]
    identity = jnp.eye(width, dtype=jnp.float32)
    trace_value = jnp.einsum('bii->b', fisher)
    damped = fisher + (DAMPING * trace_value)[:, None, None] * identity
    total = jnp.einsum('bii->b', damped)
    iterate = identity[None] / total[:, None, None]
    for _ in range(STEPS):
        product = jnp.einsum('bij,bjk->bik', damped, iterate, precision=lax.Precision.HIGHEST)
        iterate = jnp.einsum('bij,bjk->bik', iterate, 2.0 * identity - product, precision=lax.Precision.HIGHEST)
    return iterate

def reference(gradients, projection_seed, target_features):
    seed_value = projection_seed[0]

    def add_shard(shard, accumulated):
        first_col = (shard * COORD_DEV).astype(jnp.int32)
        grad_slab = lax.dynamic_slice_in_dim(gradients, first_col, COORD_DEV, 1)
        matrix = hashed(seed_value, first_col, COORD_DEV, 0, FEATS, COORDS)
        return accumulated + jnp.dot(grad_slab, matrix, preferred_element_type=jnp.float32)
    summed = lax.fori_loop(0, N_PARAM, add_shard, jnp.zeros((EXAMPLES, FEATS), jnp.float32))
    features = lax.optimization_barrier(summed.astype(jnp.bfloat16))
    widened = features.astype(jnp.float32).reshape(EXAMPLES, FEATS // BLOCK, BLOCK)
    fisher = jnp.einsum('ebi,ebj->bij', widened, widened, precision=lax.Precision.HIGHEST) / EXAMPLES
    inverse = newton_inverse(fisher)
    inverse_bf = lax.optimization_barrier(inverse.astype(jnp.bfloat16)).astype(jnp.float32)
    conditioned = jnp.einsum('ebm,bmj->ebj', widened, inverse_bf, precision=lax.Precision.HIGHEST)
    conditioned = conditioned.astype(jnp.bfloat16).reshape(EXAMPLES, FEATS)
    return jnp.dot(target_features, conditioned.T, preferred_element_type=jnp.float32)
```

```python
import functools
import math

import jax
import jax.numpy as jnp
from jax import lax
from jax.experimental import pallas as pl
from jax.experimental.pallas import tpu as pltpu
from jax.sharding import PartitionSpec as P

FEATS = 4096
BLOCK = 128
STEPS = 10
DAMPING = 0.001
MESH = pl.DeviceIdType.MESH


def row_part(start, shape, seed_value):
    row = start + lax.broadcasted_iota(jnp.int32, shape, 0)
    mixed = row * 73856093 ^ seed_value * 83492791
    return mixed ^ jnp.right_shift(mixed, 13) ^ jnp.int32(-(2**31))


def col_part(start, shape):
    col = start + lax.broadcasted_iota(jnp.int32, shape, 1)
    mixed = col * 19349663
    return mixed ^ jnp.right_shift(mixed, 13)


def centred(rows, cols):
    mixed = (rows ^ cols) * 1274126177
    mixed = mixed ^ jnp.left_shift(mixed, 16)
    return jnp.right_shift(mixed, 16).astype(jnp.float32).astype(jnp.bfloat16)


def body(
    sizes, seed_ref, grad_ref, target_ref, out_ref,
    grads, rows_tab, cols_tab, tile_a, tile_b, targets, acc, mine, xs, xr, zs, zr, ys, feats,
    pre, pre_all, part, part_bf, part_in,
    local_sem, grad_sem, x_sem, z_sem, y_sem, pre_sem, score_sem,
):
    n_param, n_ex, exam_dev, coord_dev, target_rows, depth = sizes
    n_far, n_y = n_param // 2, n_ex // 2
    width = n_y * BLOCK
    p, e = lax.axis_index("param"), lax.axis_index("ex")
    z, x, y, c = p // 2, p % 2, e // 2, e % 2
    pair = 2 * exam_dev
    total_coords = coord_dev * n_param

    def copy(src, dst, sem, slot, pp, ee):
        return pltpu.make_async_remote_copy(
            src_ref=src, dst_ref=dst, send_sem=sem.at[0, slot], recv_sem=sem.at[1, slot],
            device_id=(pp, ee), device_id_type=MESH,
        )

    own_rows = pl.ds(pl.multiple_of(c * exam_dev, exam_dev), exam_dev)
    load_grad = pltpu.make_async_copy(grad_ref, grads.at[own_rows], local_sem.at[0])
    load_grad.start()
    own_cols = pl.ds(pl.multiple_of(p * (n_ex * BLOCK), n_ex * BLOCK), n_ex * BLOCK)
    load_target = pltpu.make_async_copy(target_ref.at[:, own_cols], targets, local_sem.at[1])
    load_target.start()

    barrier = pltpu.get_barrier_semaphore()
    for d in range(1, n_param):
        pl.semaphore_signal(barrier, inc=1, device_id=((p + d) % n_param, e), device_id_type=MESH)
    for d in range(1, n_ex):
        pl.semaphore_signal(barrier, inc=1, device_id=(p, (e + d) % n_ex), device_id_type=MESH)

    seed_value = seed_ref[0]
    rows_tab[...] = row_part(p * coord_dev, rows_tab.shape, seed_value)

    order = [("x", 0)]
    for s in range(1, n_far):
        order += [("x", s), ("m", s - 1)]
    order += [("m", n_far - 1)]

    def far(s):
        return (z + 1 + s) % n_far

    for i, (kind, s) in enumerate(order):
        to = far(s) * 2 + (1 - x if kind == "x" else x)
        cols_tab[i] = col_part(to * (n_ex * BLOCK) + c * width, (8, width))
    cols_tab[len(order)] = cols_tab[0]

    tiles = coord_dev // depth

    def make(tile, t, i):
        start = pl.multiple_of(t * depth, depth)
        cols = cols_tab[i]
        for w in range(0, width, BLOCK):
            col = cols[0:1, w : w + BLOCK]
            tile[:, w : w + BLOCK] = centred(rows_tab[pl.ds(start, depth), :], col)

    def use(tile, t):
        start = pl.multiple_of(t * depth, depth)
        acc[...] += jnp.dot(
            grads[:, pl.ds(start, depth)], tile[...], preferred_element_type=jnp.float32
        )

    make(tile_a, 0, 0)
    pl.semaphore_wait(barrier, n_param - 1 + n_ex - 1)
    swap = copy(grad_ref, grads.at[own_rows], grad_sem, 0, p, e + 1 - 2 * c)
    swap.start()
    load_grad.wait()
    swap.wait()

    x_copies, z_copies = [], []
    for i, (kind, s) in enumerate(order):
        acc[...] = jnp.zeros_like(acc)

        def step(t, carry):
            make(tile_b, 2 * t + 1, i)
            use(tile_a, 2 * t)
            later = (2 * t + 2) // tiles
            make(tile_a, 2 * t + 2 - later * tiles, i + later)
            use(tile_b, 2 * t + 1)
            return carry

        lax.fori_loop(0, tiles // 2, step, 0)
        if kind == "x":
            xs[s] = acc[...].astype(jnp.bfloat16)
            copy_x = copy(xs.at[s], xr.at[s], x_sem, s, p + 1 - 2 * x, e)
            copy_x.start()
            x_copies.append(copy_x)
        else:
            x_copies[s].wait_recv()
            both = acc[...] + xr[s].astype(jnp.float32)
            if s < n_far - 1:
                zs[s] = both.astype(jnp.bfloat16)
                copy_z = copy(zs.at[s], zr.at[s], z_sem, s, far(s) * 2 + x, e)
                copy_z.start()
                z_copies.append(copy_z)
            else:
                mine[...] = both

    total = mine[...]
    for s in range(n_far - 1):
        z_copies[s].wait_recv()
        total = total + zr[s].astype(jnp.float32)
    total = (total * (math.sqrt(3.0 / total_coords) / 32768.0)).astype(jnp.bfloat16)
    for k in range(n_y):
        ys[k] = total[:, k * BLOCK : (k + 1) * BLOCK]
    my_pair = pl.ds(pl.multiple_of(y * pair, pair), pair)
    y_copies = []
    for d in range(1, n_y):
        there = (y + d) % n_y
        copy_y = copy(ys.at[there], feats.at[my_pair], y_sem, d - 1, p, there * 2 + c)
        copy_y.start()
        y_copies.append(copy_y)
    feats[my_pair, :] = ys[y]
    for copy_y in y_copies:
        copy_y.wait_recv()

    fisher = lax.dot_general(
        feats[...], feats[...], (((0,), (0,)), ((), ())), preferred_element_type=jnp.float32
    ) / (n_ex * exam_dev)
    eye = (
        lax.broadcasted_iota(jnp.int32, (BLOCK, BLOCK), 0)
        == lax.broadcasted_iota(jnp.int32, (BLOCK, BLOCK), 1)
    ).astype(jnp.float32)

    def trace(square):
        return jnp.sum(jnp.sum(square * eye, axis=0, keepdims=True), axis=1, keepdims=True)

    damped = fisher + (DAMPING * trace(fisher)) * eye
    inverse = eye / trace(damped)
    gap = eye - damped / trace(damped)
    for step_index in range(STEPS):
        if step_index < STEPS - 1:
            both = jnp.dot(
                jnp.concatenate([inverse, gap], 0), gap,
                precision=lax.Precision.HIGHEST, preferred_element_type=jnp.float32,
            )
            inverse, gap = inverse + both[:BLOCK], both[BLOCK:]
        else:
            inverse = inverse + jnp.dot(
                inverse, gap, precision=lax.Precision.HIGHEST, preferred_element_type=jnp.float32
            )
    pre[...] = jnp.dot(
        feats[...], inverse.astype(jnp.bfloat16), preferred_element_type=jnp.float32
    ).astype(jnp.bfloat16)

    slot = pl.ds(pl.multiple_of((c * n_y + y) * BLOCK, BLOCK), BLOCK)
    pre_copies = []
    for d in range(1, n_ex):
        there = (e + d) % n_ex
        src = pre.at[pl.ds(pl.multiple_of(there * exam_dev, exam_dev), exam_dev)]
        copy_p = copy(src, pre_all.at[:, slot], pre_sem, d - 1, p, there)
        copy_p.start()
        pre_copies.append(copy_p)
    pre_all[:, slot] = pre[pl.ds(pl.multiple_of(e * exam_dev, exam_dev), exam_dev), :]
    load_target.wait()
    for copy_p in pre_copies:
        copy_p.wait_recv()

    part[...] = lax.dot_general(
        targets[...], pre_all[...], (((1,), (1,)), ((), ())), preferred_element_type=jnp.float32
    )
    part_bf[...] = part[...].astype(jnp.bfloat16)
    t_dev = target_rows // n_param
    score_copies = []
    for d in range(1, n_param):
        there = (p + d) % n_param
        src = part_bf.at[pl.ds(pl.multiple_of(there * t_dev, t_dev), t_dev)]
        copy_s = copy(src, part_in.at[d - 1], score_sem, d - 1, there, e)
        copy_s.start()
        score_copies.append(copy_s)
    result = part[pl.ds(pl.multiple_of(p * t_dev, t_dev), t_dev), :]
    for d in range(1, n_param):
        score_copies[d - 1].wait_recv()
        result = result + part_in[d - 1].astype(jnp.float32)
    out_ref[...] = result
    for group in (x_copies, z_copies, y_copies, pre_copies, score_copies):
        for one in group:
            one.wait_send()


def fused(gradients, projection_seed, target_features):
    n_param, n_ex = lax.axis_size("param"), lax.axis_size("ex")
    exam_dev, coord_dev = gradients.shape
    target_rows = target_features.shape[0]
    n_far, n_y = n_param // 2, n_ex // 2
    width, pair = n_y * BLOCK, 2 * exam_dev
    t_dev = target_rows // n_param
    depth = math.gcd(coord_dev // 2, 1024)
    bf, f32 = jnp.bfloat16, jnp.float32
    sizes = (n_param, n_ex, exam_dev, coord_dev, target_rows, depth)
    dma = pltpu.SemaphoreType.DMA
    return pl.pallas_call(
        functools.partial(body, sizes),
        out_shape=jax.ShapeDtypeStruct((t_dev, exam_dev), f32),
        in_specs=[
            pl.BlockSpec(memory_space=pltpu.SMEM),
            pl.BlockSpec(memory_space=pl.ANY),
            pl.BlockSpec(memory_space=pl.ANY),
        ],
        out_specs=pl.BlockSpec(memory_space=pltpu.VMEM),
        scratch_shapes=[
            pltpu.VMEM((pair, coord_dev), bf),
            pltpu.VMEM((coord_dev, BLOCK), jnp.int32),
            pltpu.VMEM((n_param + 1, 8, width), jnp.int32),
            pltpu.VMEM((depth, width), bf),
            pltpu.VMEM((depth, width), bf),
            pltpu.VMEM((target_rows, n_ex * BLOCK), bf),
            pltpu.VMEM((pair, width), f32),
            pltpu.VMEM((pair, width), f32),
            pltpu.VMEM((n_far, pair, width), bf),
            pltpu.VMEM((n_far, pair, width), bf),
            pltpu.VMEM((n_far, pair, width), bf),
            pltpu.VMEM((n_far, pair, width), bf),
            pltpu.VMEM((n_y, pair, BLOCK), bf),
            pltpu.VMEM((n_ex * exam_dev, BLOCK), bf),
            pltpu.VMEM((n_ex * exam_dev, BLOCK), bf),
            pltpu.VMEM((exam_dev, n_ex * BLOCK), bf),
            pltpu.VMEM((target_rows, exam_dev), f32),
            pltpu.VMEM((target_rows, exam_dev), bf),
            pltpu.VMEM((n_param - 1, t_dev, exam_dev), bf),
            dma((2,)),
            dma((2, 1)),
            dma((2, n_far)),
            dma((2, n_far)),
            dma((2, n_y)),
            dma((2, n_ex)),
            dma((2, n_param)),
        ],
        compiler_params=pltpu.CompilerParams(
            collective_id=0, has_side_effects=True, vmem_limit_bytes=40 * 2**20
        ),
    )(projection_seed, gradients, target_features)


def kernel_fits(gradients, target_features):
    n_param, n_ex = lax.axis_size("param"), lax.axis_size("ex")
    exam_dev, coord_dev = gradients.shape
    return (
        n_param * n_ex * BLOCK == FEATS
        and n_param % 2 == 0
        and n_ex % 2 == 0
        and exam_dev % BLOCK == 0
        and coord_dev % 2048 == 0
        and target_features.shape[0] % (16 * n_param) == 0
    )


def partner_2(array, axis, distance):
    return lax.ppermute(array, axis, [(i, i ^ 1 << distance) for i in range(lax.axis_size(axis))])


def hashed(seed_value, row_start, row_count, col_start, col_count, total_coords):
    row_index = (row_start + lax.iota(jnp.int32, row_count)).reshape(row_count, 1)
    col_index = (col_start + lax.iota(jnp.int32, col_count)).reshape(1, col_count)
    mixed = row_index * 73856093 ^ col_index * 19349663 ^ seed_value * 83492791
    mixed = mixed ^ jnp.right_shift(mixed, 13)
    mixed = mixed * 1274126177
    mixed = mixed ^ jnp.right_shift(mixed, 16)
    uniform_value = (mixed & 65535).astype(jnp.float32) * (1.0 / 65536.0)
    return ((2.0 * uniform_value - 1.0) * math.sqrt(3.0 / total_coords)).astype(jnp.bfloat16)


def newton_inverse(fisher):
    width = fisher.shape[1]
    identity = jnp.eye(width, dtype=jnp.float32)
    trace_value = jnp.einsum("bii->b", fisher)
    damped = fisher + (DAMPING * trace_value)[:, None, None] * identity
    total = jnp.einsum("bii->b", damped)
    iterate = identity[None] / total[:, None, None]
    for _ in range(STEPS):
        product = jnp.einsum("bij,bjk->bik", damped, iterate, precision=lax.Precision.HIGHEST)
        iterate = jnp.einsum(
            "bij,bjk->bik", iterate, 2.0 * identity - product, precision=lax.Precision.HIGHEST
        )
    return iterate


def to_targets(partial_scores):
    return lax.all_to_all(partial_scores, "param", split_axis=0, concat_axis=1, tiled=True)


def on_device(gradients, projection_seed, target_features):
    if kernel_fits(gradients, target_features):
        return fused(gradients, projection_seed, target_features)
    seed_value = projection_seed[0]
    my_index = lax.axis_index("param")
    param_count = lax.axis_size("param")
    exam_dev, coord_dev = gradients.shape
    total_coords = coord_dev * param_count
    row_start = my_index * coord_dev
    examples_total = exam_dev * lax.axis_size("ex")
    feats_owned = FEATS // param_count
    piece_width = math.gcd(feats_owned * lax.axis_size("param"), 512)

    def project_piece(col_start):
        matrix = hashed(seed_value, row_start, coord_dev, col_start, piece_width, total_coords)
        return jnp.dot(gradients, matrix, preferred_element_type=jnp.float32).T

    starts = piece_width * lax.iota(jnp.int32, feats_owned * lax.axis_size("param") // piece_width)
    pieces = lax.map(project_piece, starts)
    owned = lax.psum_scatter(
        pieces.reshape(feats_owned * lax.axis_size("param"), exam_dev),
        "param",
        scatter_dimension=0,
        tiled=True,
    ).astype(jnp.bfloat16)
    if feats_owned < BLOCK:
        partner = partner_2(owned, "param", 0)
        is_lower = my_index % 2 == 0
        block_rows = jnp.concatenate(
            [jnp.where(is_lower, owned, partner), jnp.where(is_lower, partner, owned)], 0
        )
    else:
        block_rows = owned
    block_total = block_rows.shape[0] // BLOCK
    blocks = block_rows.reshape(block_total, BLOCK, exam_dev)
    partial_fisher = jnp.einsum("bie,bje->bij", blocks, blocks, preferred_element_type=jnp.float32)
    fisher = lax.psum(partial_fisher, "ex") / examples_total
    inverse_bf = newton_inverse(fisher).astype(jnp.bfloat16)
    conditioned = jnp.einsum("bmj,bme->bje", inverse_bf, blocks, preferred_element_type=jnp.float32)
    conditioned = conditioned.astype(jnp.bfloat16).reshape(block_rows.shape[0], exam_dev)
    if feats_owned < BLOCK:
        conditioned = lax.dynamic_slice_in_dim(
            conditioned, my_index % 2 * feats_owned, feats_owned, 0
        )
    example_rows = lax.all_to_all(conditioned, "param", split_axis=1, concat_axis=0, tiled=True)
    return to_targets(jnp.dot(target_features, example_rows, preferred_element_type=jnp.float32))


def solution(mesh):
    placed = (P("ex", "param"), P(), P())
    return jax.shard_map(
        on_device, mesh=mesh, in_specs=placed, out_specs=P("param", "ex"), check_vma=False
    )
```

```python
import functools
import math

import jax
import jax.numpy as jnp
from jax import lax
from jax.experimental import pallas as pl
from jax.experimental.pallas import tpu as pltpu
from jax.sharding import PartitionSpec as P

FEATS = 4096
BLOCK = 128
STEPS = 10
DAMPING = 0.001
PIECE = 64
MESH = pl.DeviceIdType.MESH


def row_part(start, shape, seed_value):
    row = start + lax.broadcasted_iota(jnp.int32, shape, 0)
    mixed = row * 73856093 ^ seed_value * 83492791
    return mixed ^ jnp.right_shift(mixed, 13) ^ jnp.int32(-(2**31))


def col_part(start, shape):
    col = start + lax.broadcasted_iota(jnp.int32, shape, 1)
    mixed = col * 19349663
    return mixed ^ jnp.right_shift(mixed, 13)


def centred(rows, cols):
    mixed = (rows ^ cols) * 1274126177
    mixed = mixed ^ jnp.left_shift(mixed, 16)
    return jnp.right_shift(mixed, 16).astype(jnp.float32)


def body(
    sizes, seed_ref, grad_ref, target_ref, out_ref,
    grads, rows_tab, cols_tab, proj_a, proj_b, targets, acc, mine, xs, xr, zs, zr, ys, feats,
    pre, pre_all, part, part_bf, part_in,
    local_sem, grad_sem, x_sem, z_sem, y_sem, pre_sem, score_sem,
):
    n_param, n_ex, exam_dev, coord_dev, target_rows, depth = sizes
    n_far, n_y = n_param // 2, n_ex // 2
    width = n_y * BLOCK
    p, e = lax.axis_index("param"), lax.axis_index("ex")
    z, x, y, c = p // 2, p % 2, e // 2, e % 2
    pair = 2 * exam_dev
    total_coords = coord_dev * n_param

    def copy(src, dst, sem, slot, pp, ee):
        return pltpu.make_async_remote_copy(
            src_ref=src, dst_ref=dst, send_sem=sem.at[0, slot], recv_sem=sem.at[1, slot],
            device_id=(pp, ee), device_id_type=MESH,
        )

    own_rows = pl.ds(pl.multiple_of(c * exam_dev, exam_dev), exam_dev)
    load_grad = pltpu.make_async_copy(grad_ref, grads.at[own_rows], local_sem.at[0])
    load_grad.start()
    own_cols = pl.ds(pl.multiple_of(p * (n_ex * BLOCK), n_ex * BLOCK), n_ex * BLOCK)
    load_target = pltpu.make_async_copy(target_ref.at[:, own_cols], targets, local_sem.at[1])
    load_target.start()

    barrier = pltpu.get_barrier_semaphore()
    for d in range(1, n_param):
        pl.semaphore_signal(barrier, inc=1, device_id=((p + d) % n_param, e), device_id_type=MESH)
    for d in range(1, n_ex):
        pl.semaphore_signal(barrier, inc=1, device_id=(p, (e + d) % n_ex), device_id_type=MESH)

    seed_value = seed_ref[0]
    rows_tab[...] = row_part(p * coord_dev, rows_tab.shape, seed_value)

    order = [("x", 0)]
    for s in range(1, n_far):
        order += [("x", s), ("m", s - 1)]
    order += [("m", n_far - 1)]

    def far(s):
        return (z + 1 + s) % n_far

    for i, (kind, s) in enumerate(order):
        to = far(s) * 2 + (1 - x if kind == "x" else x)
        cols_tab[i] = col_part(to * (n_ex * BLOCK) + c * width, (8, width))

    tiles = coord_dev // depth
    projs = (proj_a, proj_b)

    def make(proj, t, i):
        start = pl.multiple_of(t * depth, depth)
        for k in range(0, depth, PIECE):
            here = pl.ds(pl.multiple_of(start + k, PIECE), PIECE)
            rows = rows_tab[here, :].reshape(PIECE // 8, 8, BLOCK)
            for w in range(0, width, BLOCK):
                values = centred(rows, cols_tab[i, :, w : w + BLOCK][None])
                proj[here, w : w + BLOCK] = values.reshape(PIECE, BLOCK).astype(jnp.bfloat16)

    def use(proj, t):
        here = pl.ds(pl.multiple_of(t * depth, depth), depth)
        acc[...] += jnp.dot(grads[:, here], proj[here, :], preferred_element_type=jnp.float32)

    def swap(t):
        here = pl.ds(pl.multiple_of(t * depth, depth), depth)
        return copy(grad_ref.at[:, here], grads.at[own_rows, here], grad_sem, t, p, e + 1 - 2 * c)

    pl.semaphore_wait(barrier, n_param - 1 + n_ex - 1)

    def first(t, carry):
        swap(t).start()
        return carry

    def ahead(t, carry):
        make(projs[0], t, 0)
        return carry

    lax.fori_loop(0, tiles, first, 0)
    lax.fori_loop(0, tiles, ahead, 0)
    load_grad.wait()

    x_copies, z_copies = [], []
    for i, (kind, s) in enumerate(order):
        acc[...] = jnp.zeros_like(acc)

        def step(t, carry):
            if i == 0:
                swap(t).wait()
            if i + 1 < len(order):
                make(projs[(i + 1) % 2], t, i + 1)
            use(projs[i % 2], t)
            return carry

        lax.fori_loop(0, tiles, step, 0)
        if kind == "x":
            xs[s] = acc[...].astype(jnp.bfloat16)
            copy_x = copy(xs.at[s], xr.at[s], x_sem, s, p + 1 - 2 * x, e)
            copy_x.start()
            x_copies.append(copy_x)
        else:
            x_copies[s].wait_recv()
            both = acc[...] + xr[s].astype(jnp.float32)
            if s < n_far - 1:
                zs[s] = both.astype(jnp.bfloat16)
                copy_z = copy(zs.at[s], zr.at[s], z_sem, s, far(s) * 2 + x, e)
                copy_z.start()
                z_copies.append(copy_z)
            else:
                mine[...] = both

    total = mine[...]
    for s in range(n_far - 1):
        z_copies[s].wait_recv()
        total = total + zr[s].astype(jnp.float32)
    total = (total * (math.sqrt(3.0 / total_coords) / 32768.0)).astype(jnp.bfloat16)
    for k in range(n_y):
        ys[k] = total[:, k * BLOCK : (k + 1) * BLOCK]
    my_pair = pl.ds(pl.multiple_of(y * pair, pair), pair)
    y_copies = []
    for d in range(1, n_y):
        there = (y + d) % n_y
        copy_y = copy(ys.at[there], feats.at[my_pair], y_sem, d - 1, p, there * 2 + c)
        copy_y.start()
        y_copies.append(copy_y)
    feats[my_pair, :] = ys[y]
    for copy_y in y_copies:
        copy_y.wait_recv()

    fisher = lax.dot_general(
        feats[...], feats[...], (((0,), (0,)), ((), ())), preferred_element_type=jnp.float32
    ) / (n_ex * exam_dev)
    eye = (
        lax.broadcasted_iota(jnp.int32, (BLOCK, BLOCK), 0)
        == lax.broadcasted_iota(jnp.int32, (BLOCK, BLOCK), 1)
    ).astype(jnp.float32)

    def trace(square):
        return jnp.sum(jnp.sum(square * eye, axis=0, keepdims=True), axis=1, keepdims=True)

    damped = fisher + (DAMPING * trace(fisher)) * eye
    inverse = eye / trace(damped)
    gap = eye - damped / trace(damped)
    for step_index in range(STEPS):
        if step_index < STEPS - 1:
            both = jnp.dot(
                jnp.concatenate([inverse, gap], 0), gap,
                precision=lax.Precision.HIGHEST, preferred_element_type=jnp.float32,
            )
            inverse, gap = inverse + both[:BLOCK], both[BLOCK:]
        else:
            inverse = inverse + jnp.dot(
                inverse, gap, precision=lax.Precision.HIGHEST, preferred_element_type=jnp.float32
            )
    pre[...] = jnp.dot(
        feats[...], inverse.astype(jnp.bfloat16), preferred_element_type=jnp.float32
    ).astype(jnp.bfloat16)

    slot = pl.ds(pl.multiple_of((c * n_y + y) * BLOCK, BLOCK), BLOCK)
    pre_copies = []
    for d in range(1, n_ex):
        there = (e + d) % n_ex
        src = pre.at[pl.ds(pl.multiple_of(there * exam_dev, exam_dev), exam_dev)]
        copy_p = copy(src, pre_all.at[:, slot], pre_sem, d - 1, p, there)
        copy_p.start()
        pre_copies.append(copy_p)
    pre_all[:, slot] = pre[pl.ds(pl.multiple_of(e * exam_dev, exam_dev), exam_dev), :]
    load_target.wait()
    for copy_p in pre_copies:
        copy_p.wait_recv()

    part[...] = lax.dot_general(
        targets[...], pre_all[...], (((1,), (1,)), ((), ())), preferred_element_type=jnp.float32
    )
    part_bf[...] = part[...].astype(jnp.bfloat16)
    t_dev = target_rows // n_param
    score_copies = []
    for d in range(1, n_param):
        there = (p + d) % n_param
        src = part_bf.at[pl.ds(pl.multiple_of(there * t_dev, t_dev), t_dev)]
        copy_s = copy(src, part_in.at[d - 1], score_sem, d - 1, there, e)
        copy_s.start()
        score_copies.append(copy_s)
    result = part[pl.ds(pl.multiple_of(p * t_dev, t_dev), t_dev), :]
    for d in range(1, n_param):
        score_copies[d - 1].wait_recv()
        result = result + part_in[d - 1].astype(jnp.float32)
    out_ref[...] = result
    for group in (x_copies, z_copies, y_copies, pre_copies, score_copies):
        for one in group:
            one.wait_send()


def fused(gradients, projection_seed, target_features):
    n_param, n_ex = lax.axis_size("param"), lax.axis_size("ex")
    exam_dev, coord_dev = gradients.shape
    target_rows = target_features.shape[0]
    n_far, n_y = n_param // 2, n_ex // 2
    width, pair = n_y * BLOCK, 2 * exam_dev
    t_dev = target_rows // n_param
    depth = math.gcd(coord_dev, 1024)
    bf, f32 = jnp.bfloat16, jnp.float32
    sizes = (n_param, n_ex, exam_dev, coord_dev, target_rows, depth)
    dma = pltpu.SemaphoreType.DMA
    return pl.pallas_call(
        functools.partial(body, sizes),
        out_shape=jax.ShapeDtypeStruct((t_dev, exam_dev), f32),
        in_specs=[
            pl.BlockSpec(memory_space=pltpu.SMEM),
            pl.BlockSpec(memory_space=pl.ANY),
            pl.BlockSpec(memory_space=pl.ANY),
        ],
        out_specs=pl.BlockSpec(memory_space=pltpu.VMEM),
        scratch_shapes=[
            pltpu.VMEM((pair, coord_dev), bf),
            pltpu.VMEM((coord_dev, BLOCK), jnp.int32),
            pltpu.VMEM((n_param, 8, width), jnp.int32),
            pltpu.VMEM((coord_dev, width), bf),
            pltpu.VMEM((coord_dev, width), bf),
            pltpu.VMEM((target_rows, n_ex * BLOCK), bf),
            pltpu.VMEM((pair, width), f32),
            pltpu.VMEM((pair, width), f32),
            pltpu.VMEM((n_far, pair, width), bf),
            pltpu.VMEM((n_far, pair, width), bf),
            pltpu.VMEM((n_far, pair, width), bf),
            pltpu.VMEM((n_far, pair, width), bf),
            pltpu.VMEM((n_y, pair, BLOCK), bf),
            pltpu.VMEM((n_ex * exam_dev, BLOCK), bf),
            pltpu.VMEM((n_ex * exam_dev, BLOCK), bf),
            pltpu.VMEM((exam_dev, n_ex * BLOCK), bf),
            pltpu.VMEM((target_rows, exam_dev), f32),
            pltpu.VMEM((target_rows, exam_dev), bf),
            pltpu.VMEM((n_param - 1, t_dev, exam_dev), bf),
            dma((2,)),
            dma((2, coord_dev // depth)),
            dma((2, n_far)),
            dma((2, n_far)),
            dma((2, n_y)),
            dma((2, n_ex)),
            dma((2, n_param)),
        ],
        compiler_params=pltpu.CompilerParams(
            collective_id=0, has_side_effects=True, vmem_limit_bytes=58 * 2**20
        ),
    )(projection_seed, gradients, target_features)


def kernel_fits(gradients, target_features):
    n_param, n_ex = lax.axis_size("param"), lax.axis_size("ex")
    exam_dev, coord_dev = gradients.shape
    return (
        n_param * n_ex * BLOCK == FEATS
        and n_param % 2 == 0
        and n_ex % 2 == 0
        and exam_dev % BLOCK == 0
        and coord_dev % 2048 == 0
        and target_features.shape[0] % (16 * n_param) == 0
    )


def partner_2(array, axis, distance):
    return lax.ppermute(array, axis, [(i, i ^ 1 << distance) for i in range(lax.axis_size(axis))])


def hashed(seed_value, row_start, row_count, col_start, col_count, total_coords):
    row_index = (row_start + lax.iota(jnp.int32, row_count)).reshape(row_count, 1)
    col_index = (col_start + lax.iota(jnp.int32, col_count)).reshape(1, col_count)
    mixed = row_index * 73856093 ^ col_index * 19349663 ^ seed_value * 83492791
    mixed = mixed ^ jnp.right_shift(mixed, 13)
    mixed = mixed * 1274126177
    mixed = mixed ^ jnp.right_shift(mixed, 16)
    uniform_value = (mixed & 65535).astype(jnp.float32) * (1.0 / 65536.0)
    return ((2.0 * uniform_value - 1.0) * math.sqrt(3.0 / total_coords)).astype(jnp.bfloat16)


def newton_inverse(fisher):
    width = fisher.shape[1]
    identity = jnp.eye(width, dtype=jnp.float32)
    trace_value = jnp.einsum("bii->b", fisher)
    damped = fisher + (DAMPING * trace_value)[:, None, None] * identity
    total = jnp.einsum("bii->b", damped)
    iterate = identity[None] / total[:, None, None]
    for _ in range(STEPS):
        product = jnp.einsum("bij,bjk->bik", damped, iterate, precision=lax.Precision.HIGHEST)
        iterate = jnp.einsum(
            "bij,bjk->bik", iterate, 2.0 * identity - product, precision=lax.Precision.HIGHEST
        )
    return iterate


def to_targets(partial_scores):
    return lax.all_to_all(partial_scores, "param", split_axis=0, concat_axis=1, tiled=True)


def on_device(gradients, projection_seed, target_features):
    if kernel_fits(gradients, target_features):
        return fused(gradients, projection_seed, target_features)
    seed_value = projection_seed[0]
    my_index = lax.axis_index("param")
    param_count = lax.axis_size("param")
    exam_dev, coord_dev = gradients.shape
    total_coords = coord_dev * param_count
    row_start = my_index * coord_dev
    examples_total = exam_dev * lax.axis_size("ex")
    feats_owned = FEATS // param_count
    piece_width = math.gcd(feats_owned * lax.axis_size("param"), 512)

    def project_piece(col_start):
        matrix = hashed(seed_value, row_start, coord_dev, col_start, piece_width, total_coords)
        return jnp.dot(gradients, matrix, preferred_element_type=jnp.float32).T

    starts = piece_width * lax.iota(jnp.int32, feats_owned * lax.axis_size("param") // piece_width)
    pieces = lax.map(project_piece, starts)
    owned = lax.psum_scatter(
        pieces.reshape(feats_owned * lax.axis_size("param"), exam_dev),
        "param",
        scatter_dimension=0,
        tiled=True,
    ).astype(jnp.bfloat16)
    if feats_owned < BLOCK:
        partner = partner_2(owned, "param", 0)
        is_lower = my_index % 2 == 0
        block_rows = jnp.concatenate(
            [jnp.where(is_lower, owned, partner), jnp.where(is_lower, partner, owned)], 0
        )
    else:
        block_rows = owned
    block_total = block_rows.shape[0] // BLOCK
    blocks = block_rows.reshape(block_total, BLOCK, exam_dev)
    partial_fisher = jnp.einsum("bie,bje->bij", blocks, blocks, preferred_element_type=jnp.float32)
    fisher = lax.psum(partial_fisher, "ex") / examples_total
    inverse_bf = newton_inverse(fisher).astype(jnp.bfloat16)
    conditioned = jnp.einsum("bmj,bme->bje", inverse_bf, blocks, preferred_element_type=jnp.float32)
    conditioned = conditioned.astype(jnp.bfloat16).reshape(block_rows.shape[0], exam_dev)
    if feats_owned < BLOCK:
        conditioned = lax.dynamic_slice_in_dim(
            conditioned, my_index % 2 * feats_owned, feats_owned, 0
        )
    example_rows = lax.all_to_all(conditioned, "param", split_axis=1, concat_axis=0, tiled=True)
    return to_targets(jnp.dot(target_features, example_rows, preferred_element_type=jnp.float32))


def solution(mesh):
    placed = (P("ex", "param"), P(), P())
    return jax.shard_map(
        on_device, mesh=mesh, in_specs=placed, out_specs=P("param", "ex"), check_vma=False
    )
```

```python
import functools
import math

import jax
import jax.numpy as jnp
from jax import lax
from jax.experimental import pallas as pl
from jax.experimental.pallas import tpu as pltpu
from jax.sharding import PartitionSpec as P

FEATS = 4096
BLOCK = 128
STEPS = 10
DAMPING = 0.001
PIECE = 64
MESH = pl.DeviceIdType.MESH


def row_part(start, shape, seed_value):
    row = start + lax.broadcasted_iota(jnp.int32, shape, 0)
    mixed = row * 73856093 ^ seed_value * 83492791
    return mixed ^ jnp.right_shift(mixed, 13) ^ jnp.int32(-(2**31))


def col_part(start, shape):
    col = start + lax.broadcasted_iota(jnp.int32, shape, 1)
    mixed = col * 19349663
    return mixed ^ jnp.right_shift(mixed, 13)


def centred(rows, cols):
    mixed = (rows ^ cols) * 1274126177
    mixed = mixed ^ jnp.left_shift(mixed, 16)
    return jnp.right_shift(mixed, 16).astype(jnp.float32)


def body(
    sizes, seed_ref, grad_ref, target_ref, out_ref,
    grads, rows_tab, cols_tab, proj_a, proj_b, targets, acc, mine, xs, xr, zs, zr, ys, feats,
    pre, pre_all, part, part_bf, part_in,
    local_sem, grad_sem, x_sem, z_sem, y_sem, pre_sem, score_sem,
):
    n_param, n_ex, exam_dev, coord_dev, target_rows, depth = sizes
    n_far, n_y = n_param // 2, n_ex // 2
    width = n_y * BLOCK
    p, e = lax.axis_index("param"), lax.axis_index("ex")
    z, x, y, c = p // 2, p % 2, e // 2, e % 2
    pair = 2 * exam_dev
    total_coords = coord_dev * n_param

    def copy(src, dst, sem, slot, pp, ee):
        return pltpu.make_async_remote_copy(
            src_ref=src, dst_ref=dst, send_sem=sem.at[0, slot], recv_sem=sem.at[1, slot],
            device_id=(pp, ee), device_id_type=MESH,
        )

    own_rows = pl.ds(pl.multiple_of(c * exam_dev, exam_dev), exam_dev)
    load_grad = pltpu.make_async_copy(grad_ref, grads.at[own_rows], local_sem.at[0])
    load_grad.start()
    own_cols = pl.ds(pl.multiple_of(p * (n_ex * BLOCK), n_ex * BLOCK), n_ex * BLOCK)
    load_target = pltpu.make_async_copy(target_ref.at[:, own_cols], targets, local_sem.at[1])
    load_target.start()

    barrier = pltpu.get_barrier_semaphore()
    for d in range(1, n_param):
        pl.semaphore_signal(barrier, inc=1, device_id=((p + d) % n_param, e), device_id_type=MESH)
    for d in range(1, n_ex):
        pl.semaphore_signal(barrier, inc=1, device_id=(p, (e + d) % n_ex), device_id_type=MESH)

    tiles = coord_dev // depth
    projs = (proj_a, proj_b)

    order = [("x", s) for s in range(n_far - 1)] + [("m", s) for s in range(n_far - 1)]
    order += [("x", n_far - 1), ("m", n_far - 1)]

    def far(s):
        return (z + 1 + s) % n_far

    def make(proj, t, i):
        start = pl.multiple_of(t * depth, depth)
        for k in range(0, depth, PIECE):
            here = pl.ds(pl.multiple_of(start + k, PIECE), PIECE)
            rows = rows_tab[here, :].reshape(PIECE // 8, 8, BLOCK)
            for w in range(0, width, BLOCK):
                values = centred(rows, cols_tab[i, :, w : w + BLOCK][None])
                proj[here, w : w + BLOCK] = values.reshape(PIECE, BLOCK).astype(jnp.bfloat16)

    def use(proj, t):
        here = pl.ds(pl.multiple_of(t * depth, depth), depth)
        acc[...] += jnp.dot(grads[:, here], proj[here, :], preferred_element_type=jnp.float32)

    def swap(t):
        here = pl.ds(pl.multiple_of(t * depth, depth), depth)
        return copy(grad_ref.at[:, here], grads.at[own_rows, here], grad_sem, t, p, e + 1 - 2 * c)

    def first(t, carry):
        swap(t).start()
        return carry

    def ahead(t, carry):
        make(projs[0], t, 0)
        return carry

    pl.semaphore_wait(barrier, n_param - 1 + n_ex - 1)
    lax.fori_loop(0, tiles, first, 0)
    seed_value = seed_ref[0]
    rows_tab[...] = row_part(p * coord_dev, rows_tab.shape, seed_value)
    for i, (kind, s) in enumerate(order):
        to = far(s) * 2 + (1 - x if kind == "x" else x)
        cols_tab[i] = col_part(to * (n_ex * BLOCK) + c * width, (8, width))

    lax.fori_loop(0, tiles, ahead, 0)
    load_grad.wait()

    x_copies, z_copies = [], []
    for i, (kind, s) in enumerate(order):
        acc[...] = jnp.zeros_like(acc)

        def step(t, carry):
            if i == 0:
                swap(t).wait()
            if i + 1 < len(order):
                make(projs[(i + 1) % 2], t, i + 1)
            use(projs[i % 2], t)
            return carry

        lax.fori_loop(0, tiles, step, 0)
        if kind == "x":
            xs[s] = acc[...].astype(jnp.bfloat16)
            copy_x = copy(xs.at[s], xr.at[s], x_sem, s, p + 1 - 2 * x, e)
            copy_x.start()
            x_copies.append(copy_x)
        else:
            x_copies[s].wait_recv()
            both = acc[...] + xr[s].astype(jnp.float32)
            if s < n_far - 1:
                zs[s] = both.astype(jnp.bfloat16)
                copy_z = copy(zs.at[s], zr.at[s], z_sem, s, far(s) * 2 + x, e)
                copy_z.start()
                z_copies.append(copy_z)
            else:
                mine[...] = both

    total = mine[...]
    for s in range(n_far - 1):
        z_copies[s].wait_recv()
        total = total + zr[s].astype(jnp.float32)
    total = (total * (math.sqrt(3.0 / total_coords) / 32768.0)).astype(jnp.bfloat16)
    for k in range(n_y):
        ys[k] = total[:, k * BLOCK : (k + 1) * BLOCK]
    my_pair = pl.ds(pl.multiple_of(y * pair, pair), pair)
    y_copies = []
    for d in range(1, n_y):
        there = (y + d) % n_y
        copy_y = copy(ys.at[there], feats.at[my_pair], y_sem, d - 1, p, there * 2 + c)
        copy_y.start()
        y_copies.append(copy_y)
    feats[my_pair, :] = ys[y]
    for copy_y in y_copies:
        copy_y.wait_recv()

    fisher = lax.dot_general(
        feats[...], feats[...], (((0,), (0,)), ((), ())), preferred_element_type=jnp.float32
    ) / (n_ex * exam_dev)
    eye = (
        lax.broadcasted_iota(jnp.int32, (BLOCK, BLOCK), 0)
        == lax.broadcasted_iota(jnp.int32, (BLOCK, BLOCK), 1)
    ).astype(jnp.float32)

    def trace(square):
        return jnp.sum(jnp.sum(square * eye, axis=0, keepdims=True), axis=1, keepdims=True)

    damped = fisher + (DAMPING * trace(fisher)) * eye
    inverse = eye / trace(damped)
    gap = eye - damped / trace(damped)
    for step_index in range(STEPS):
        if step_index < STEPS - 1:
            both = jnp.dot(
                jnp.concatenate([inverse, gap], 0), gap,
                precision=lax.Precision.HIGHEST, preferred_element_type=jnp.float32,
            )
            inverse, gap = inverse + both[:BLOCK], both[BLOCK:]
        else:
            inverse = inverse + jnp.dot(
                inverse, gap, precision=lax.Precision.HIGHEST, preferred_element_type=jnp.float32
            )
    pre[...] = jnp.dot(
        feats[...], inverse.astype(jnp.bfloat16), preferred_element_type=jnp.float32
    ).astype(jnp.bfloat16)

    slot = pl.ds(pl.multiple_of((c * n_y + y) * BLOCK, BLOCK), BLOCK)
    pre_copies = []
    for d in range(1, n_ex):
        there = (e + d) % n_ex
        src = pre.at[pl.ds(pl.multiple_of(there * exam_dev, exam_dev), exam_dev)]
        copy_p = copy(src, pre_all.at[:, slot], pre_sem, d - 1, p, there)
        copy_p.start()
        pre_copies.append(copy_p)
    pre_all[:, slot] = pre[pl.ds(pl.multiple_of(e * exam_dev, exam_dev), exam_dev), :]
    load_target.wait()
    for copy_p in pre_copies:
        copy_p.wait_recv()

    part[...] = lax.dot_general(
        targets[...], pre_all[...], (((1,), (1,)), ((), ())), preferred_element_type=jnp.float32
    )
    part_bf[...] = part[...].astype(jnp.bfloat16)
    t_dev = target_rows // n_param
    score_copies = []
    for d in range(1, n_param):
        there = (p + d) % n_param
        src = part_bf.at[pl.ds(pl.multiple_of(there * t_dev, t_dev), t_dev)]
        copy_s = copy(src, part_in.at[d - 1], score_sem, d - 1, there, e)
        copy_s.start()
        score_copies.append(copy_s)
    result = part[pl.ds(pl.multiple_of(p * t_dev, t_dev), t_dev), :]
    for d in range(1, n_param):
        score_copies[d - 1].wait_recv()
        result = result + part_in[d - 1].astype(jnp.float32)
    out_ref[...] = result
    for group in (x_copies, z_copies, y_copies, pre_copies, score_copies):
        for one in group:
            one.wait_send()


def fused(gradients, projection_seed, target_features):
    n_param, n_ex = lax.axis_size("param"), lax.axis_size("ex")
    exam_dev, coord_dev = gradients.shape
    target_rows = target_features.shape[0]
    n_far, n_y = n_param // 2, n_ex // 2
    width, pair = n_y * BLOCK, 2 * exam_dev
    t_dev = target_rows // n_param
    depth = math.gcd(coord_dev, 2048)
    bf, f32 = jnp.bfloat16, jnp.float32
    sizes = (n_param, n_ex, exam_dev, coord_dev, target_rows, depth)
    dma = pltpu.SemaphoreType.DMA
    return pl.pallas_call(
        functools.partial(body, sizes),
        out_shape=jax.ShapeDtypeStruct((t_dev, exam_dev), f32),
        in_specs=[
            pl.BlockSpec(memory_space=pltpu.SMEM),
            pl.BlockSpec(memory_space=pl.ANY),
            pl.BlockSpec(memory_space=pl.ANY),
        ],
        out_specs=pl.BlockSpec(memory_space=pltpu.VMEM),
        scratch_shapes=[
            pltpu.VMEM((pair, coord_dev), bf),
            pltpu.VMEM((coord_dev, BLOCK), jnp.int32),
            pltpu.VMEM((n_param, 8, width), jnp.int32),
            pltpu.VMEM((coord_dev, width), bf),
            pltpu.VMEM((coord_dev, width), bf),
            pltpu.VMEM((target_rows, n_ex * BLOCK), bf),
            pltpu.VMEM((pair, width), f32),
            pltpu.VMEM((pair, width), f32),
            pltpu.VMEM((n_far, pair, width), bf),
            pltpu.VMEM((n_far, pair, width), bf),
            pltpu.VMEM((n_far, pair, width), bf),
            pltpu.VMEM((n_far, pair, width), bf),
            pltpu.VMEM((n_y, pair, BLOCK), bf),
            pltpu.VMEM((n_ex * exam_dev, BLOCK), bf),
            pltpu.VMEM((n_ex * exam_dev, BLOCK), bf),
            pltpu.VMEM((exam_dev, n_ex * BLOCK), bf),
            pltpu.VMEM((target_rows, exam_dev), f32),
            pltpu.VMEM((target_rows, exam_dev), bf),
            pltpu.VMEM((n_param - 1, t_dev, exam_dev), bf),
            dma((2,)),
            dma((2, coord_dev // depth)),
            dma((2, n_far)),
            dma((2, n_far)),
            dma((2, n_y)),
            dma((2, n_ex)),
            dma((2, n_param)),
        ],
        compiler_params=pltpu.CompilerParams(
            collective_id=0, has_side_effects=True, vmem_limit_bytes=58 * 2**20
        ),
    )(projection_seed, gradients, target_features)


def kernel_fits(gradients, target_features):
    n_param, n_ex = lax.axis_size("param"), lax.axis_size("ex")
    exam_dev, coord_dev = gradients.shape
    return (
        n_param * n_ex * BLOCK == FEATS
        and n_param % 2 == 0
        and n_ex % 2 == 0
        and exam_dev % BLOCK == 0
        and coord_dev % 2048 == 0
        and target_features.shape[0] % (16 * n_param) == 0
    )


def partner_2(array, axis, distance):
    return lax.ppermute(array, axis, [(i, i ^ 1 << distance) for i in range(lax.axis_size(axis))])


def hashed(seed_value, row_start, row_count, col_start, col_count, total_coords):
    row_index = (row_start + lax.iota(jnp.int32, row_count)).reshape(row_count, 1)
    col_index = (col_start + lax.iota(jnp.int32, col_count)).reshape(1, col_count)
    mixed = row_index * 73856093 ^ col_index * 19349663 ^ seed_value * 83492791
    mixed = mixed ^ jnp.right_shift(mixed, 13)
    mixed = mixed * 1274126177
    mixed = mixed ^ jnp.right_shift(mixed, 16)
    uniform_value = (mixed & 65535).astype(jnp.float32) * (1.0 / 65536.0)
    return ((2.0 * uniform_value - 1.0) * math.sqrt(3.0 / total_coords)).astype(jnp.bfloat16)


def newton_inverse(fisher):
    width = fisher.shape[1]
    identity = jnp.eye(width, dtype=jnp.float32)
    trace_value = jnp.einsum("bii->b", fisher)
    damped = fisher + (DAMPING * trace_value)[:, None, None] * identity
    total = jnp.einsum("bii->b", damped)
    iterate = identity[None] / total[:, None, None]
    for _ in range(STEPS):
        product = jnp.einsum("bij,bjk->bik", damped, iterate, precision=lax.Precision.HIGHEST)
        iterate = jnp.einsum(
            "bij,bjk->bik", iterate, 2.0 * identity - product, precision=lax.Precision.HIGHEST
        )
    return iterate


def to_targets(partial_scores):
    return lax.all_to_all(partial_scores, "param", split_axis=0, concat_axis=1, tiled=True)


def on_device(gradients, projection_seed, target_features):
    if kernel_fits(gradients, target_features):
        return fused(gradients, projection_seed, target_features)
    seed_value = projection_seed[0]
    my_index = lax.axis_index("param")
    param_count = lax.axis_size("param")
    exam_dev, coord_dev = gradients.shape
    total_coords = coord_dev * param_count
    row_start = my_index * coord_dev
    examples_total = exam_dev * lax.axis_size("ex")
    feats_owned = FEATS // param_count
    piece_width = math.gcd(feats_owned * lax.axis_size("param"), 512)

    def project_piece(col_start):
        matrix = hashed(seed_value, row_start, coord_dev, col_start, piece_width, total_coords)
        return jnp.dot(gradients, matrix, preferred_element_type=jnp.float32).T

    starts = piece_width * lax.iota(jnp.int32, feats_owned * lax.axis_size("param") // piece_width)
    pieces = lax.map(project_piece, starts)
    owned = lax.psum_scatter(
        pieces.reshape(feats_owned * lax.axis_size("param"), exam_dev),
        "param",
        scatter_dimension=0,
        tiled=True,
    ).astype(jnp.bfloat16)
    if feats_owned < BLOCK:
        partner = partner_2(owned, "param", 0)
        is_lower = my_index % 2 == 0
        block_rows = jnp.concatenate(
            [jnp.where(is_lower, owned, partner), jnp.where(is_lower, partner, owned)], 0
        )
    else:
        block_rows = owned
    block_total = block_rows.shape[0] // BLOCK
    blocks = block_rows.reshape(block_total, BLOCK, exam_dev)
    partial_fisher = jnp.einsum("bie,bje->bij", blocks, blocks, preferred_element_type=jnp.float32)
    fisher = lax.psum(partial_fisher, "ex") / examples_total
    inverse_bf = newton_inverse(fisher).astype(jnp.bfloat16)
    conditioned = jnp.einsum("bmj,bme->bje", inverse_bf, blocks, preferred_element_type=jnp.float32)
    conditioned = conditioned.astype(jnp.bfloat16).reshape(block_rows.shape[0], exam_dev)
    if feats_owned < BLOCK:
        conditioned = lax.dynamic_slice_in_dim(
            conditioned, my_index % 2 * feats_owned, feats_owned, 0
        )
    example_rows = lax.all_to_all(conditioned, "param", split_axis=1, concat_axis=0, tiled=True)
    return to_targets(jnp.dot(target_features, example_rows, preferred_element_type=jnp.float32))


def solution(mesh):
    placed = (P("ex", "param"), P(), P())
    return jax.shard_map(
        on_device, mesh=mesh, in_specs=placed, out_specs=P("param", "ex"), check_vma=False
    )
```

```python
import functools
import math

import jax
import jax.numpy as jnp
from jax import lax
from jax.experimental import pallas as pl
from jax.experimental.pallas import tpu as pltpu
from jax.sharding import PartitionSpec as P

FEATS = 4096
BLOCK = 128
STEPS = 10
DAMPING = 0.001
PIECE = 64
MESH = pl.DeviceIdType.MESH


def row_part(start, shape, seed_value):
    row = start + lax.broadcasted_iota(jnp.int32, shape, 0)
    mixed = row * 73856093 ^ seed_value * 83492791
    return mixed ^ jnp.right_shift(mixed, 13) ^ jnp.int32(-(2**31))


def col_part(start, shape):
    col = start + lax.broadcasted_iota(jnp.int32, shape, 1)
    mixed = col * 19349663
    return mixed ^ jnp.right_shift(mixed, 13)


def centred(rows, cols):
    mixed = (rows ^ cols) * 1274126177
    mixed = mixed ^ jnp.left_shift(mixed, 16)
    return jnp.right_shift(mixed, 16).astype(jnp.float32)


def body(
    sizes, seed_ref, grad_ref, target_ref, out_ref,
    grads, rows_tab, cols_tab, proj_a, proj_b, targets, acc, mine, xs, xr, zs, zr, ys, feats,
    pre, pre_all, part, part_bf, part_in,
    local_sem, grad_sem, x_sem, z_sem, y_sem, pre_sem, score_sem,
):
    n_param, n_ex, exam_dev, coord_dev, target_rows, depth = sizes
    n_far, n_y = n_param // 2, n_ex // 2
    width = n_y * BLOCK
    p, e = lax.axis_index("param"), lax.axis_index("ex")
    z, x, y, c = p // 2, p % 2, e // 2, e % 2
    pair = 2 * exam_dev
    total_coords = coord_dev * n_param

    def copy(src, dst, sem, slot, pp, ee):
        return pltpu.make_async_remote_copy(
            src_ref=src, dst_ref=dst, send_sem=sem.at[0, slot], recv_sem=sem.at[1, slot],
            device_id=(pp, ee), device_id_type=MESH,
        )

    own_rows = pl.ds(pl.multiple_of(c * exam_dev, exam_dev), exam_dev)
    load_grad = pltpu.make_async_copy(grad_ref, grads.at[own_rows], local_sem.at[0])
    load_grad.start()
    own_cols = pl.ds(pl.multiple_of(p * (n_ex * BLOCK), n_ex * BLOCK), n_ex * BLOCK)
    load_target = pltpu.make_async_copy(target_ref.at[:, own_cols], targets, local_sem.at[1])
    load_target.start()

    barrier = pltpu.get_barrier_semaphore()
    for d in range(1, n_param):
        pl.semaphore_signal(barrier, inc=1, device_id=((p + d) % n_param, e), device_id_type=MESH)
    for d in range(1, n_ex):
        pl.semaphore_signal(barrier, inc=1, device_id=(p, (e + d) % n_ex), device_id_type=MESH)

    tiles = coord_dev // depth

    def far(s):
        return (z + 1 + s) % n_far

    def make(proj, t, i):
        start = pl.multiple_of(t * depth, depth)
        for k in range(0, depth, PIECE):
            here = pl.ds(pl.multiple_of(start + k, PIECE), PIECE)
            rows = rows_tab[here, :].reshape(PIECE // 8, 8, BLOCK)
            for w in range(0, width, BLOCK):
                values = centred(rows, cols_tab[i, :, w : w + BLOCK][None])
                proj[here, w : w + BLOCK] = values.reshape(PIECE, BLOCK).astype(jnp.bfloat16)

    def use(proj, t):
        here = pl.ds(pl.multiple_of(t * depth, depth), depth)
        acc[...] += jnp.dot(grads[:, here], proj[here, :], preferred_element_type=jnp.float32)

    def swap(t):
        here = pl.ds(pl.multiple_of(t * depth, depth), depth)
        return copy(grad_ref.at[:, here], grads.at[own_rows, here], grad_sem, t, p, e + 1 - 2 * c)

    def first(t, carry):
        swap(t).start()
        return carry

    def ahead(t, carry):
        make(proj_a, t, 0)
        return carry

    pl.semaphore_wait(barrier, n_param - 1 + n_ex - 1)
    lax.fori_loop(0, tiles, first, 0)
    seed_value = seed_ref[0]
    rows_tab[...] = row_part(p * coord_dev, rows_tab.shape, seed_value)
    for i in range(n_param):
        to = far(i // 2) * 2 + (x if i % 2 else 1 - x)
        cols_tab[i] = col_part(to * (n_ex * BLOCK) + c * width, (8, width))
    lax.fori_loop(0, tiles, ahead, 0)
    load_grad.wait()

    def run(i, now, later):
        acc[...] = jnp.zeros_like(acc)

        def step(t, carry):
            @pl.when(i == 0)
            def _():
                swap(t).wait()

            if later is not None:
                make(later, t, i + 1)
            use(now, t)
            return carry

        lax.fori_loop(0, tiles, step, 0)

    def x_copy(s):
        return copy(xs.at[s], xr.at[s], x_sem, s, p + 1 - 2 * x, e)

    def z_copy(s):
        return copy(zs.at[s], zr.at[s], z_sem, s, far(s) * 2 + x, e)

    def send_x(s):
        xs[s] = acc[...].astype(jnp.bfloat16)
        x_copy(s).start()

    def send_z(s):
        x_copy(s).wait_recv()
        zs[s] = (mine[...] + xr[s].astype(jnp.float32)).astype(jnp.bfloat16)
        z_copy(s).start()

    def both_chunks(s, carry):
        run(2 * s, proj_a, proj_b)
        send_x(s)

        @pl.when(s > 0)
        def _():
            send_z(s - 1)

        run(2 * s + 1, proj_b, proj_a)
        mine[...] = acc[...]
        return carry

    lax.fori_loop(0, n_far - 1, both_chunks, 0)
    run(n_param - 2, proj_a, proj_b)
    send_x(n_far - 1)
    send_z(n_far - 2)
    run(n_param - 1, proj_b, None)
    x_copy(n_far - 1).wait_recv()
    total = acc[...] + xr[n_far - 1].astype(jnp.float32)
    for s in range(n_far - 1):
        z_copy(s).wait_recv()
        total = total + zr[s].astype(jnp.float32)
    total = (total * (math.sqrt(3.0 / total_coords) / 32768.0)).astype(jnp.bfloat16)
    for k in range(n_y):
        ys[k] = total[:, k * BLOCK : (k + 1) * BLOCK]
    my_pair = pl.ds(pl.multiple_of(y * pair, pair), pair)
    y_copies = []
    for d in range(1, n_y):
        there = (y + d) % n_y
        copy_y = copy(ys.at[there], feats.at[my_pair], y_sem, d - 1, p, there * 2 + c)
        copy_y.start()
        y_copies.append(copy_y)
    feats[my_pair, :] = ys[y]
    for copy_y in y_copies:
        copy_y.wait_recv()

    fisher = lax.dot_general(
        feats[...], feats[...], (((0,), (0,)), ((), ())), preferred_element_type=jnp.float32
    ) / (n_ex * exam_dev)
    eye = (
        lax.broadcasted_iota(jnp.int32, (BLOCK, BLOCK), 0)
        == lax.broadcasted_iota(jnp.int32, (BLOCK, BLOCK), 1)
    ).astype(jnp.float32)

    def trace(square):
        return jnp.sum(jnp.sum(square * eye, axis=0, keepdims=True), axis=1, keepdims=True)

    damped = fisher + (DAMPING * trace(fisher)) * eye
    inverse = eye / trace(damped)
    gap = eye - damped / trace(damped)
    for step_index in range(STEPS):
        if step_index < STEPS - 1:
            both = jnp.dot(
                jnp.concatenate([inverse, gap], 0), gap,
                precision=lax.Precision.HIGHEST, preferred_element_type=jnp.float32,
            )
            inverse, gap = inverse + both[:BLOCK], both[BLOCK:]
        else:
            inverse = inverse + jnp.dot(
                inverse, gap, precision=lax.Precision.HIGHEST, preferred_element_type=jnp.float32
            )
    pre[...] = jnp.dot(
        feats[...], inverse.astype(jnp.bfloat16), preferred_element_type=jnp.float32
    ).astype(jnp.bfloat16)

    slot = pl.ds(pl.multiple_of((c * n_y + y) * BLOCK, BLOCK), BLOCK)
    pre_copies = []
    for d in range(1, n_ex):
        there = (e + d) % n_ex
        src = pre.at[pl.ds(pl.multiple_of(there * exam_dev, exam_dev), exam_dev)]
        copy_p = copy(src, pre_all.at[:, slot], pre_sem, d - 1, p, there)
        copy_p.start()
        pre_copies.append(copy_p)
    pre_all[:, slot] = pre[pl.ds(pl.multiple_of(e * exam_dev, exam_dev), exam_dev), :]
    load_target.wait()
    for copy_p in pre_copies:
        copy_p.wait_recv()

    part[...] = lax.dot_general(
        targets[...], pre_all[...], (((1,), (1,)), ((), ())), preferred_element_type=jnp.float32
    )
    part_bf[...] = part[...].astype(jnp.bfloat16)
    t_dev = target_rows // n_param
    score_copies = []
    for d in range(1, n_param):
        there = (p + d) % n_param
        src = part_bf.at[pl.ds(pl.multiple_of(there * t_dev, t_dev), t_dev)]
        copy_s = copy(src, part_in.at[d - 1], score_sem, d - 1, there, e)
        copy_s.start()
        score_copies.append(copy_s)
    result = part[pl.ds(pl.multiple_of(p * t_dev, t_dev), t_dev), :]
    for d in range(1, n_param):
        score_copies[d - 1].wait_recv()
        result = result + part_in[d - 1].astype(jnp.float32)
    out_ref[...] = result
    sent = [x_copy(s) for s in range(n_far)] + [z_copy(s) for s in range(n_far - 1)]
    for one in sent + y_copies + pre_copies + score_copies:
        one.wait_send()


def fused(gradients, projection_seed, target_features):
    n_param, n_ex = lax.axis_size("param"), lax.axis_size("ex")
    exam_dev, coord_dev = gradients.shape
    target_rows = target_features.shape[0]
    n_far, n_y = n_param // 2, n_ex // 2
    width, pair = n_y * BLOCK, 2 * exam_dev
    t_dev = target_rows // n_param
    depth = math.gcd(coord_dev, 2048)
    bf, f32 = jnp.bfloat16, jnp.float32
    sizes = (n_param, n_ex, exam_dev, coord_dev, target_rows, depth)
    dma = pltpu.SemaphoreType.DMA
    return pl.pallas_call(
        functools.partial(body, sizes),
        out_shape=jax.ShapeDtypeStruct((t_dev, exam_dev), f32),
        in_specs=[
            pl.BlockSpec(memory_space=pltpu.SMEM),
            pl.BlockSpec(memory_space=pl.ANY),
            pl.BlockSpec(memory_space=pl.ANY),
        ],
        out_specs=pl.BlockSpec(memory_space=pltpu.VMEM),
        scratch_shapes=[
            pltpu.VMEM((pair, coord_dev), bf),
            pltpu.VMEM((coord_dev, BLOCK), jnp.int32),
            pltpu.VMEM((n_param, 8, width), jnp.int32),
            pltpu.VMEM((coord_dev, width), bf),
            pltpu.VMEM((coord_dev, width), bf),
            pltpu.VMEM((target_rows, n_ex * BLOCK), bf),
            pltpu.VMEM((pair, width), f32),
            pltpu.VMEM((pair, width), f32),
            pltpu.VMEM((n_far, pair, width), bf),
            pltpu.VMEM((n_far, pair, width), bf),
            pltpu.VMEM((n_far, pair, width), bf),
            pltpu.VMEM((n_far, pair, width), bf),
            pltpu.VMEM((n_y, pair, BLOCK), bf),
            pltpu.VMEM((n_ex * exam_dev, BLOCK), bf),
            pltpu.VMEM((n_ex * exam_dev, BLOCK), bf),
            pltpu.VMEM((exam_dev, n_ex * BLOCK), bf),
            pltpu.VMEM((target_rows, exam_dev), f32),
            pltpu.VMEM((target_rows, exam_dev), bf),
            pltpu.VMEM((n_param - 1, t_dev, exam_dev), bf),
            dma((2,)),
            dma((2, coord_dev // depth)),
            dma((2, n_far)),
            dma((2, n_far)),
            dma((2, n_y)),
            dma((2, n_ex)),
            dma((2, n_param)),
        ],
        compiler_params=pltpu.CompilerParams(
            collective_id=0, has_side_effects=True, vmem_limit_bytes=58 * 2**20
        ),
    )(projection_seed, gradients, target_features)


def kernel_fits(gradients, target_features):
    n_param, n_ex = lax.axis_size("param"), lax.axis_size("ex")
    exam_dev, coord_dev = gradients.shape
    return (
        n_param * n_ex * BLOCK == FEATS
        and n_param % 2 == 0
        and n_param >= 4
        and n_ex % 2 == 0
        and exam_dev % BLOCK == 0
        and coord_dev % 2048 == 0
        and target_features.shape[0] % (16 * n_param) == 0
    )


def partner_2(array, axis, distance):
    return lax.ppermute(array, axis, [(i, i ^ 1 << distance) for i in range(lax.axis_size(axis))])


def hashed(seed_value, row_start, row_count, col_start, col_count, total_coords):
    row_index = (row_start + lax.iota(jnp.int32, row_count)).reshape(row_count, 1)
    col_index = (col_start + lax.iota(jnp.int32, col_count)).reshape(1, col_count)
    mixed = row_index * 73856093 ^ col_index * 19349663 ^ seed_value * 83492791
    mixed = mixed ^ jnp.right_shift(mixed, 13)
    mixed = mixed * 1274126177
    mixed = mixed ^ jnp.right_shift(mixed, 16)
    uniform_value = (mixed & 65535).astype(jnp.float32) * (1.0 / 65536.0)
    return ((2.0 * uniform_value - 1.0) * math.sqrt(3.0 / total_coords)).astype(jnp.bfloat16)


def newton_inverse(fisher):
    width = fisher.shape[1]
    identity = jnp.eye(width, dtype=jnp.float32)
    trace_value = jnp.einsum("bii->b", fisher)
    damped = fisher + (DAMPING * trace_value)[:, None, None] * identity
    total = jnp.einsum("bii->b", damped)
    iterate = identity[None] / total[:, None, None]
    for _ in range(STEPS):
        product = jnp.einsum("bij,bjk->bik", damped, iterate, precision=lax.Precision.HIGHEST)
        iterate = jnp.einsum(
            "bij,bjk->bik", iterate, 2.0 * identity - product, precision=lax.Precision.HIGHEST
        )
    return iterate


def to_targets(partial_scores):
    return lax.all_to_all(partial_scores, "param", split_axis=0, concat_axis=1, tiled=True)


def on_device(gradients, projection_seed, target_features):
    if kernel_fits(gradients, target_features):
        return fused(gradients, projection_seed, target_features)
    seed_value = projection_seed[0]
    my_index = lax.axis_index("param")
    param_count = lax.axis_size("param")
    exam_dev, coord_dev = gradients.shape
    total_coords = coord_dev * param_count
    row_start = my_index * coord_dev
    examples_total = exam_dev * lax.axis_size("ex")
    feats_owned = FEATS // param_count
    piece_width = math.gcd(feats_owned * lax.axis_size("param"), 512)

    def project_piece(col_start):
        matrix = hashed(seed_value, row_start, coord_dev, col_start, piece_width, total_coords)
        return jnp.dot(gradients, matrix, preferred_element_type=jnp.float32).T

    starts = piece_width * lax.iota(jnp.int32, feats_owned * lax.axis_size("param") // piece_width)
    pieces = lax.map(project_piece, starts)
    owned = lax.psum_scatter(
        pieces.reshape(feats_owned * lax.axis_size("param"), exam_dev),
        "param",
        scatter_dimension=0,
        tiled=True,
    ).astype(jnp.bfloat16)
    if feats_owned < BLOCK:
        partner = partner_2(owned, "param", 0)
        is_lower = my_index % 2 == 0
        block_rows = jnp.concatenate(
            [jnp.where(is_lower, owned, partner), jnp.where(is_lower, partner, owned)], 0
        )
    else:
        block_rows = owned
    block_total = block_rows.shape[0] // BLOCK
    blocks = block_rows.reshape(block_total, BLOCK, exam_dev)
    partial_fisher = jnp.einsum("bie,bje->bij", blocks, blocks, preferred_element_type=jnp.float32)
    fisher = lax.psum(partial_fisher, "ex") / examples_total
    inverse_bf = newton_inverse(fisher).astype(jnp.bfloat16)
    conditioned = jnp.einsum("bmj,bme->bje", inverse_bf, blocks, preferred_element_type=jnp.float32)
    conditioned = conditioned.astype(jnp.bfloat16).reshape(block_rows.shape[0], exam_dev)
    if feats_owned < BLOCK:
        conditioned = lax.dynamic_slice_in_dim(
            conditioned, my_index % 2 * feats_owned, feats_owned, 0
        )
    example_rows = lax.all_to_all(conditioned, "param", split_axis=1, concat_axis=0, tiled=True)
    return to_targets(jnp.dot(target_features, example_rows, preferred_element_type=jnp.float32))


def solution(mesh):
    placed = (P("ex", "param"), P(), P())
    return jax.shard_map(
        on_device, mesh=mesh, in_specs=placed, out_specs=P("param", "ex"), check_vma=False
    )
```

```python
import functools
import math

import jax
import jax.numpy as jnp
from jax import lax
from jax.experimental import pallas as pl
from jax.experimental.pallas import tpu as pltpu
from jax.sharding import PartitionSpec as P

FEATS = 4096
BLOCK = 128
STEPS = 10
DAMPING = 0.001
PIECE = 64
MESH = pl.DeviceIdType.MESH


def row_part(start, shape, seed_value):
    row = start + lax.broadcasted_iota(jnp.int32, shape, 0)
    mixed = row * 73856093 ^ seed_value * 83492791
    return mixed ^ jnp.right_shift(mixed, 13) ^ jnp.int32(-(2**31))


def col_part(start, shape):
    col = start + lax.broadcasted_iota(jnp.int32, shape, 1)
    mixed = col * 19349663
    return mixed ^ jnp.right_shift(mixed, 13)


def centred(rows, cols):
    mixed = (rows ^ cols) * 1274126177
    mixed = mixed ^ jnp.left_shift(mixed, 16)
    return jnp.right_shift(mixed, 16).astype(jnp.float32)


def split(values):
    high = values.astype(jnp.bfloat16)
    return high, (values - high.astype(jnp.float32)).astype(jnp.bfloat16)


def body(
    sizes, seed_ref, grad_ref, target_ref, out_ref,
    grads, rows_tab, cols_tab, proj_a, proj_b, targets, acc, mine, xs, xr, zs, zr, ys, feats,
    pre, pre_all, part, part_bf, part_in,
    local_sem, grad_sem, x_sem, z_sem, y_sem, pre_sem, score_sem,
):
    n_param, n_ex, exam_dev, coord_dev, target_rows, depth = sizes
    n_far, n_y = n_param // 2, n_ex // 2
    width = n_y * BLOCK
    p, e = lax.axis_index("param"), lax.axis_index("ex")
    z, x, y, c = p // 2, p % 2, e // 2, e % 2
    pair = 2 * exam_dev
    total_coords = coord_dev * n_param

    def copy(src, dst, sem, slot, pp, ee):
        return pltpu.make_async_remote_copy(
            src_ref=src, dst_ref=dst, send_sem=sem.at[0, slot], recv_sem=sem.at[1, slot],
            device_id=(pp, ee), device_id_type=MESH,
        )

    own_rows = pl.ds(pl.multiple_of(c * exam_dev, exam_dev), exam_dev)
    load_grad = pltpu.make_async_copy(grad_ref, grads.at[own_rows], local_sem.at[0])
    load_grad.start()
    own_cols = pl.ds(pl.multiple_of(p * (n_ex * BLOCK), n_ex * BLOCK), n_ex * BLOCK)
    load_target = pltpu.make_async_copy(target_ref.at[:, own_cols], targets, local_sem.at[1])
    load_target.start()

    barrier = pltpu.get_barrier_semaphore()
    for d in range(1, n_param):
        pl.semaphore_signal(barrier, inc=1, device_id=((p + d) % n_param, e), device_id_type=MESH)
    for d in range(1, n_ex):
        pl.semaphore_signal(barrier, inc=1, device_id=(p, (e + d) % n_ex), device_id_type=MESH)

    tiles = coord_dev // depth
    projs = (proj_a, proj_b)

    order = [("x", s) for s in range(n_far - 1)] + [("m", s) for s in range(n_far - 1)]
    order += [("x", n_far - 1), ("m", n_far - 1)]

    def far(s):
        return (z + 1 + s) % n_far

    def make(proj, t, i):
        start = pl.multiple_of(t * depth, depth)
        for k in range(0, depth, PIECE):
            here = pl.ds(pl.multiple_of(start + k, PIECE), PIECE)
            rows = rows_tab[here, :].reshape(PIECE // 8, 8, BLOCK)
            for w in range(0, width, BLOCK):
                values = centred(rows, cols_tab[i, :, w : w + BLOCK][None])
                proj[here, w : w + BLOCK] = values.reshape(PIECE, BLOCK).astype(jnp.bfloat16)

    def use(proj, t):
        here = pl.ds(pl.multiple_of(t * depth, depth), depth)
        acc[...] += jnp.dot(grads[:, here], proj[here, :], preferred_element_type=jnp.float32)

    def swap(t):
        here = pl.ds(pl.multiple_of(t * depth, depth), depth)
        return copy(grad_ref.at[:, here], grads.at[own_rows, here], grad_sem, t, p, e + 1 - 2 * c)

    def first(t, carry):
        swap(t).start()
        return carry

    def ahead(t, carry):
        make(projs[0], t, 0)
        return carry

    pl.semaphore_wait(barrier, n_param - 1 + n_ex - 1)
    lax.fori_loop(0, tiles, first, 0)
    seed_value = seed_ref[0]
    rows_tab[...] = row_part(p * coord_dev, rows_tab.shape, seed_value)
    for i, (kind, s) in enumerate(order):
        to = far(s) * 2 + (1 - x if kind == "x" else x)
        cols_tab[i] = col_part(to * (n_ex * BLOCK) + c * width, (8, width))

    lax.fori_loop(0, tiles, ahead, 0)
    load_grad.wait()

    x_copies, z_copies = [], []
    for i, (kind, s) in enumerate(order):
        acc[...] = jnp.zeros_like(acc)

        def step(t, carry):
            if i == 0:
                swap(t).wait()
            if i + 1 < len(order):
                make(projs[(i + 1) % 2], t, i + 1)
            use(projs[i % 2], t)
            return carry

        lax.fori_loop(0, tiles, step, 0)
        if kind == "x":
            xs[s] = acc[...].astype(jnp.bfloat16)
            copy_x = copy(xs.at[s], xr.at[s], x_sem, s, p + 1 - 2 * x, e)
            copy_x.start()
            x_copies.append(copy_x)
        else:
            x_copies[s].wait_recv()
            both = acc[...] + xr[s].astype(jnp.float32)
            if s < n_far - 1:
                zs[s] = both.astype(jnp.bfloat16)
                copy_z = copy(zs.at[s], zr.at[s], z_sem, s, far(s) * 2 + x, e)
                copy_z.start()
                z_copies.append(copy_z)
            else:
                mine[...] = both

    total = mine[...]
    for s in range(n_far - 1):
        z_copies[s].wait_recv()
        total = total + zr[s].astype(jnp.float32)
    total = (total * (math.sqrt(3.0 / total_coords) / 32768.0)).astype(jnp.bfloat16)
    for k in range(n_y):
        ys[k] = total[:, k * BLOCK : (k + 1) * BLOCK]
    my_pair = pl.ds(pl.multiple_of(y * pair, pair), pair)
    y_copies = []
    for d in range(1, n_y):
        there = (y + d) % n_y
        copy_y = copy(ys.at[there], feats.at[my_pair], y_sem, d - 1, p, there * 2 + c)
        copy_y.start()
        y_copies.append(copy_y)
    feats[my_pair, :] = ys[y]
    for copy_y in y_copies:
        copy_y.wait_recv()

    fisher = lax.dot_general(
        feats[...], feats[...], (((0,), (0,)), ((), ())), preferred_element_type=jnp.float32
    ) / (n_ex * exam_dev)
    eye = (
        lax.broadcasted_iota(jnp.int32, (BLOCK, BLOCK), 0)
        == lax.broadcasted_iota(jnp.int32, (BLOCK, BLOCK), 1)
    ).astype(jnp.float32)

    def trace(square):
        return jnp.sum(jnp.sum(square * eye, axis=0, keepdims=True), axis=1, keepdims=True)

    damped = fisher + (DAMPING * trace(fisher)) * eye
    inverse = eye / trace(damped)
    gap = eye - damped / trace(damped)
    for step_index in range(STEPS):
        last = step_index == STEPS - 1
        high, low = split(inverse if last else jnp.concatenate([inverse, gap], 0))
        gap_high, gap_low = split(gap) if last else (high[BLOCK:], low[BLOCK:])
        both = jnp.dot(
            jnp.concatenate([high, low, high], 1),
            jnp.concatenate([gap_high, gap_high, gap_low], 0),
            preferred_element_type=jnp.float32,
        )
        inverse = inverse + both[:BLOCK]
        gap = both[BLOCK:]
    pre[...] = jnp.dot(
        feats[...], inverse.astype(jnp.bfloat16), preferred_element_type=jnp.float32
    ).astype(jnp.bfloat16)

    slot = pl.ds(pl.multiple_of((c * n_y + y) * BLOCK, BLOCK), BLOCK)
    pre_copies = []
    for d in range(1, n_ex):
        there = (e + d) % n_ex
        src = pre.at[pl.ds(pl.multiple_of(there * exam_dev, exam_dev), exam_dev)]
        copy_p = copy(src, pre_all.at[:, slot], pre_sem, d - 1, p, there)
        copy_p.start()
        pre_copies.append(copy_p)
    pre_all[:, slot] = pre[pl.ds(pl.multiple_of(e * exam_dev, exam_dev), exam_dev), :]
    load_target.wait()
    for copy_p in pre_copies:
        copy_p.wait_recv()

    part[...] = lax.dot_general(
        targets[...], pre_all[...], (((1,), (1,)), ((), ())), preferred_element_type=jnp.float32
    )
    part_bf[...] = part[...].astype(jnp.bfloat16)
    t_dev = target_rows // n_param
    score_copies = []
    for d in range(1, n_param):
        there = (p + d) % n_param
        src = part_bf.at[pl.ds(pl.multiple_of(there * t_dev, t_dev), t_dev)]
        copy_s = copy(src, part_in.at[d - 1], score_sem, d - 1, there, e)
        copy_s.start()
        score_copies.append(copy_s)
    result = part[pl.ds(pl.multiple_of(p * t_dev, t_dev), t_dev), :]
    for d in range(1, n_param):
        score_copies[d - 1].wait_recv()
        result = result + part_in[d - 1].astype(jnp.float32)
    out_ref[...] = result
    for group in (x_copies, z_copies, y_copies, pre_copies, score_copies):
        for one in group:
            one.wait_send()


def fused(gradients, projection_seed, target_features):
    n_param, n_ex = lax.axis_size("param"), lax.axis_size("ex")
    exam_dev, coord_dev = gradients.shape
    target_rows = target_features.shape[0]
    n_far, n_y = n_param // 2, n_ex // 2
    width, pair = n_y * BLOCK, 2 * exam_dev
    t_dev = target_rows // n_param
    depth = math.gcd(coord_dev, 4096)
    bf, f32 = jnp.bfloat16, jnp.float32
    sizes = (n_param, n_ex, exam_dev, coord_dev, target_rows, depth)
    dma = pltpu.SemaphoreType.DMA
    return pl.pallas_call(
        functools.partial(body, sizes),
        out_shape=jax.ShapeDtypeStruct((t_dev, exam_dev), f32),
        in_specs=[
            pl.BlockSpec(memory_space=pltpu.SMEM),
            pl.BlockSpec(memory_space=pl.ANY),
            pl.BlockSpec(memory_space=pl.ANY),
        ],
        out_specs=pl.BlockSpec(memory_space=pltpu.VMEM),
        scratch_shapes=[
            pltpu.VMEM((pair, coord_dev), bf),
            pltpu.VMEM((coord_dev, BLOCK), jnp.int32),
            pltpu.VMEM((n_param, 8, width), jnp.int32),
            pltpu.VMEM((coord_dev, width), bf),
            pltpu.VMEM((coord_dev, width), bf),
            pltpu.VMEM((target_rows, n_ex * BLOCK), bf),
            pltpu.VMEM((pair, width), f32),
            pltpu.VMEM((pair, width), f32),
            pltpu.VMEM((n_far, pair, width), bf),
            pltpu.VMEM((n_far, pair, width), bf),
            pltpu.VMEM((n_far, pair, width), bf),
            pltpu.VMEM((n_far, pair, width), bf),
            pltpu.VMEM((n_y, pair, BLOCK), bf),
            pltpu.VMEM((n_ex * exam_dev, BLOCK), bf),
            pltpu.VMEM((n_ex * exam_dev, BLOCK), bf),
            pltpu.VMEM((exam_dev, n_ex * BLOCK), bf),
            pltpu.VMEM((target_rows, exam_dev), f32),
            pltpu.VMEM((target_rows, exam_dev), bf),
            pltpu.VMEM((n_param - 1, t_dev, exam_dev), bf),
            dma((2,)),
            dma((2, coord_dev // depth)),
            dma((2, n_far)),
            dma((2, n_far)),
            dma((2, n_y)),
            dma((2, n_ex)),
            dma((2, n_param)),
        ],
        compiler_params=pltpu.CompilerParams(
            collective_id=0, has_side_effects=True, vmem_limit_bytes=58 * 2**20
        ),
    )(projection_seed, gradients, target_features)


def kernel_fits(gradients, target_features):
    n_param, n_ex = lax.axis_size("param"), lax.axis_size("ex")
    exam_dev, coord_dev = gradients.shape
    return (
        n_param * n_ex * BLOCK == FEATS
        and n_param % 2 == 0
        and n_ex % 2 == 0
        and exam_dev % BLOCK == 0
        and coord_dev % 2048 == 0
        and target_features.shape[0] % (16 * n_param) == 0
    )


def partner_2(array, axis, distance):
    return lax.ppermute(array, axis, [(i, i ^ 1 << distance) for i in range(lax.axis_size(axis))])


def hashed(seed_value, row_start, row_count, col_start, col_count, total_coords):
    row_index = (row_start + lax.iota(jnp.int32, row_count)).reshape(row_count, 1)
    col_index = (col_start + lax.iota(jnp.int32, col_count)).reshape(1, col_count)
    mixed = row_index * 73856093 ^ col_index * 19349663 ^ seed_value * 83492791
    mixed = mixed ^ jnp.right_shift(mixed, 13)
    mixed = mixed * 1274126177
    mixed = mixed ^ jnp.right_shift(mixed, 16)
    uniform_value = (mixed & 65535).astype(jnp.float32) * (1.0 / 65536.0)
    return ((2.0 * uniform_value - 1.0) * math.sqrt(3.0 / total_coords)).astype(jnp.bfloat16)


def newton_inverse(fisher):
    width = fisher.shape[1]
    identity = jnp.eye(width, dtype=jnp.float32)
    trace_value = jnp.einsum("bii->b", fisher)
    damped = fisher + (DAMPING * trace_value)[:, None, None] * identity
    total = jnp.einsum("bii->b", damped)
    iterate = identity[None] / total[:, None, None]
    for _ in range(STEPS):
        product = jnp.einsum("bij,bjk->bik", damped, iterate, precision=lax.Precision.HIGHEST)
        iterate = jnp.einsum(
            "bij,bjk->bik", iterate, 2.0 * identity - product, precision=lax.Precision.HIGHEST
        )
    return iterate


def to_targets(partial_scores):
    return lax.all_to_all(partial_scores, "param", split_axis=0, concat_axis=1, tiled=True)


def on_device(gradients, projection_seed, target_features):
    if kernel_fits(gradients, target_features):
        return fused(gradients, projection_seed, target_features)
    seed_value = projection_seed[0]
    my_index = lax.axis_index("param")
    param_count = lax.axis_size("param")
    exam_dev, coord_dev = gradients.shape
    total_coords = coord_dev * param_count
    row_start = my_index * coord_dev
    examples_total = exam_dev * lax.axis_size("ex")
    feats_owned = FEATS // param_count
    piece_width = math.gcd(feats_owned * lax.axis_size("param"), 512)

    def project_piece(col_start):
        matrix = hashed(seed_value, row_start, coord_dev, col_start, piece_width, total_coords)
        return jnp.dot(gradients, matrix, preferred_element_type=jnp.float32).T

    starts = piece_width * lax.iota(jnp.int32, feats_owned * lax.axis_size("param") // piece_width)
    pieces = lax.map(project_piece, starts)
    owned = lax.psum_scatter(
        pieces.reshape(feats_owned * lax.axis_size("param"), exam_dev),
        "param",
        scatter_dimension=0,
        tiled=True,
    ).astype(jnp.bfloat16)
    if feats_owned < BLOCK:
        partner = partner_2(owned, "param", 0)
        is_lower = my_index % 2 == 0
        block_rows = jnp.concatenate(
            [jnp.where(is_lower, owned, partner), jnp.where(is_lower, partner, owned)], 0
        )
    else:
        block_rows = owned
    block_total = block_rows.shape[0] // BLOCK
    blocks = block_rows.reshape(block_total, BLOCK, exam_dev)
    partial_fisher = jnp.einsum("bie,bje->bij", blocks, blocks, preferred_element_type=jnp.float32)
    fisher = lax.psum(partial_fisher, "ex") / examples_total
    inverse_bf = newton_inverse(fisher).astype(jnp.bfloat16)
    conditioned = jnp.einsum("bmj,bme->bje", inverse_bf, blocks, preferred_element_type=jnp.float32)
    conditioned = conditioned.astype(jnp.bfloat16).reshape(block_rows.shape[0], exam_dev)
    if feats_owned < BLOCK:
        conditioned = lax.dynamic_slice_in_dim(
            conditioned, my_index % 2 * feats_owned, feats_owned, 0
        )
    example_rows = lax.all_to_all(conditioned, "param", split_axis=1, concat_axis=0, tiled=True)
    return to_targets(jnp.dot(target_features, example_rows, preferred_element_type=jnp.float32))


def solution(mesh):
    placed = (P("ex", "param"), P(), P())
    return jax.shard_map(
        on_device, mesh=mesh, in_specs=placed, out_specs=P("param", "ex"), check_vma=False
    )
```

```python
import functools
import math

import jax
import jax.numpy as jnp
from jax import lax
from jax.experimental import pallas as pl
from jax.experimental.pallas import tpu as pltpu
from jax.sharding import PartitionSpec as P

FEATS = 4096
BLOCK = 128
STEPS = 10
DAMPING = 0.001
PIECE = 64
PART = 1024
MESH = pl.DeviceIdType.MESH


def row_part(start, shape, seed_value):
    row = start + lax.broadcasted_iota(jnp.int32, shape, 0)
    mixed = row * 73856093 ^ seed_value * 83492791
    return mixed ^ jnp.right_shift(mixed, 13) ^ jnp.int32(-(2**31))


def col_part(start, shape):
    col = start + lax.broadcasted_iota(jnp.int32, shape, 1)
    mixed = col * 19349663
    return mixed ^ jnp.right_shift(mixed, 13)


def centred(rows, cols):
    mixed = (rows ^ cols) * 1274126177
    mixed = mixed ^ jnp.left_shift(mixed, 16)
    return jnp.right_shift(mixed, 16).astype(jnp.float32)


def split(values):
    high = values.astype(jnp.bfloat16)
    return high, (values - high.astype(jnp.float32)).astype(jnp.bfloat16)


def body(
    sizes, seed_ref, grad_ref, target_ref, out_ref,
    grads, rows_tab, cols_tab, proj_a, proj_b, targets, acc, mine, xs, xr, zs, zr, ys, feats,
    pre, pre_all, part, part_bf, part_in,
    local_sem, grad_sem, x_sem, z_sem, y_sem, pre_sem, score_sem,
):
    n_param, n_ex, exam_dev, coord_dev, target_rows, depth = sizes
    n_far, n_y = n_param // 2, n_ex // 2
    width = n_y * BLOCK
    p, e = lax.axis_index("param"), lax.axis_index("ex")
    z, x, y, c = p // 2, p % 2, e // 2, e % 2
    pair = 2 * exam_dev
    total_coords = coord_dev * n_param

    def copy(src, dst, sem, slot, pp, ee):
        return pltpu.make_async_remote_copy(
            src_ref=src, dst_ref=dst, send_sem=sem.at[0, slot], recv_sem=sem.at[1, slot],
            device_id=(pp, ee), device_id_type=MESH,
        )

    own_rows = pl.ds(pl.multiple_of(c * exam_dev, exam_dev), exam_dev)
    load_grad = pltpu.make_async_copy(grad_ref, grads.at[own_rows], local_sem.at[0])
    load_grad.start()
    own_cols = pl.ds(pl.multiple_of(p * (n_ex * BLOCK), n_ex * BLOCK), n_ex * BLOCK)
    load_target = pltpu.make_async_copy(target_ref.at[:, own_cols], targets, local_sem.at[1])
    load_target.start()

    barrier = pltpu.get_barrier_semaphore()
    for d in range(1, n_param):
        pl.semaphore_signal(barrier, inc=1, device_id=((p + d) % n_param, e), device_id_type=MESH)
    for d in range(1, n_ex):
        pl.semaphore_signal(barrier, inc=1, device_id=(p, (e + d) % n_ex), device_id_type=MESH)


    order = [("x", s) for s in range(n_far - 1)] + [("m", s) for s in range(n_far - 1)]
    order += [("x", n_far - 1), ("m", n_far - 1)]

    def far(s):
        return (z + 1 + s) % n_far

    def half(t, start, size):
        return pl.ds(pl.multiple_of(t * depth + start, size), size)

    def make(proj, t, i, start, size):
        for k in range(start, start + size, PIECE):
            rows = rows_tab[half(t, k, PIECE), :].reshape(PIECE // 8, 8, BLOCK)
            for w in range(0, width, BLOCK):
                values = centred(rows, cols_tab[i, :, w : w + BLOCK][None])
                values = values.reshape(PIECE, BLOCK).astype(jnp.bfloat16)
                proj[k : k + PIECE, w : w + BLOCK] = values

    def block(now, t, later=None, later_t=None, later_i=None):
        size = min(PART, depth)
        for start in range(0, depth, size):
            product = jnp.dot(
                grads[:, half(t, start, size)], now[start : start + size, :],
                preferred_element_type=jnp.float32,
            )
            if t == 0 and start == 0:
                acc[...] = product
            else:
                acc[...] += product
            if later is not None:
                make(later, later_t, later_i, start, size)

    def swap(t):
        here = pl.ds(t * depth, depth)
        return copy(grad_ref.at[:, here], grads.at[own_rows, here], grad_sem, t, p, e + 1 - 2 * c)

    pl.semaphore_wait(barrier, n_param - 1 + n_ex - 1)
    for t in range(2):
        swap(t).start()
    seed_value = seed_ref[0]
    rows_tab[...] = row_part(p * coord_dev, rows_tab.shape, seed_value)
    for i, (kind, s) in enumerate(order):
        to = far(s) * 2 + (1 - x if kind == "x" else x)
        cols_tab[i] = col_part(to * (n_ex * BLOCK) + c * width, (8, width))

    make(proj_a, 0, 0, 0, depth)
    load_grad.wait()

    def x_copy(s):
        return copy(xs.at[s], xr.at[s], x_sem, s, p + 1 - 2 * x, e)

    def z_copy(s):
        return copy(zs.at[s], zr.at[s], z_sem, s, far(s) * 2 + x, e)

    def swapped(t, i):
        @pl.when(i == 0)
        def _():
            swap(t).wait()

    def chunk(i, carry):
        swapped(0, i)
        block(proj_a, 0, proj_b, 1, i)
        swapped(1, i)
        block(proj_b, 1, proj_a, 0, i + 1)
        to_pair = jnp.logical_or(i < n_far - 1, i == n_param - 2)

        @pl.when(to_pair)
        def _():
            s = jnp.minimum(i, n_far - 1)
            xs[s] = acc[...].astype(jnp.bfloat16)
            x_copy(s).start()

        @pl.when(jnp.logical_not(to_pair))
        def _():
            s = i - (n_far - 1)
            x_copy(s).wait_recv()
            zs[s] = (acc[...] + xr[s].astype(jnp.float32)).astype(jnp.bfloat16)
            z_copy(s).start()

        return carry

    lax.fori_loop(0, n_param - 1, chunk, 0)
    block(proj_a, 0, proj_b, 1, n_param - 1)
    block(proj_b, 1)
    x_copy(n_far - 1).wait_recv()
    total = acc[...] + xr[n_far - 1].astype(jnp.float32)
    for s in range(n_far - 1):
        z_copy(s).wait_recv()
        total = total + zr[s].astype(jnp.float32)
    total = (total * (math.sqrt(3.0 / total_coords) / 32768.0)).astype(jnp.bfloat16)
    for k in range(n_y):
        ys[k] = total[:, k * BLOCK : (k + 1) * BLOCK]
    my_pair = pl.ds(pl.multiple_of(y * pair, pair), pair)
    y_copies = []
    for d in range(1, n_y):
        there = (y + d) % n_y
        copy_y = copy(ys.at[there], feats.at[my_pair], y_sem, d - 1, p, there * 2 + c)
        copy_y.start()
        y_copies.append(copy_y)
    feats[my_pair, :] = ys[y]
    for copy_y in y_copies:
        copy_y.wait_recv()

    fisher = lax.dot_general(
        feats[...], feats[...], (((0,), (0,)), ((), ())), preferred_element_type=jnp.float32
    ) / (n_ex * exam_dev)
    eye = (
        lax.broadcasted_iota(jnp.int32, (BLOCK, BLOCK), 0)
        == lax.broadcasted_iota(jnp.int32, (BLOCK, BLOCK), 1)
    ).astype(jnp.float32)

    def trace(square):
        return jnp.sum(jnp.sum(square * eye, axis=0, keepdims=True), axis=1, keepdims=True)

    damped = fisher + (DAMPING * trace(fisher)) * eye
    inverse = eye / trace(damped)
    gap = eye - damped / trace(damped)
    for step_index in range(STEPS):
        last = step_index == STEPS - 1
        high, low = split(inverse if last else jnp.concatenate([inverse, gap], 0))
        gap_high, gap_low = split(gap) if last else (high[BLOCK:], low[BLOCK:])
        both = jnp.dot(
            jnp.concatenate([high, low, high], 1),
            jnp.concatenate([gap_high, gap_high, gap_low], 0),
            preferred_element_type=jnp.float32,
        )
        inverse = inverse + both[:BLOCK]
        gap = both[BLOCK:]
    pre[...] = jnp.dot(
        feats[...], inverse.astype(jnp.bfloat16), preferred_element_type=jnp.float32
    ).astype(jnp.bfloat16)

    slot = pl.ds(pl.multiple_of((c * n_y + y) * BLOCK, BLOCK), BLOCK)
    pre_copies = []
    for d in range(1, n_ex):
        there = (e + d) % n_ex
        src = pre.at[pl.ds(pl.multiple_of(there * exam_dev, exam_dev), exam_dev)]
        copy_p = copy(src, pre_all.at[:, slot], pre_sem, d - 1, p, there)
        copy_p.start()
        pre_copies.append(copy_p)
    pre_all[:, slot] = pre[pl.ds(pl.multiple_of(e * exam_dev, exam_dev), exam_dev), :]
    load_target.wait()
    for copy_p in pre_copies:
        copy_p.wait_recv()

    part[...] = lax.dot_general(
        targets[...], pre_all[...], (((1,), (1,)), ((), ())), preferred_element_type=jnp.float32
    )
    part_bf[...] = part[...].astype(jnp.bfloat16)
    t_dev = target_rows // n_param
    score_copies = []
    for d in range(1, n_param):
        there = (p + d) % n_param
        src = part_bf.at[pl.ds(pl.multiple_of(there * t_dev, t_dev), t_dev)]
        copy_s = copy(src, part_in.at[d - 1], score_sem, d - 1, there, e)
        copy_s.start()
        score_copies.append(copy_s)
    result = part[pl.ds(pl.multiple_of(p * t_dev, t_dev), t_dev), :]
    for d in range(1, n_param):
        score_copies[d - 1].wait_recv()
        result = result + part_in[d - 1].astype(jnp.float32)
    out_ref[...] = result
    sent = [x_copy(s) for s in range(n_far)] + [z_copy(s) for s in range(n_far - 1)]
    for one in sent + y_copies + pre_copies + score_copies:
        one.wait_send()


def fused(gradients, projection_seed, target_features):
    n_param, n_ex = lax.axis_size("param"), lax.axis_size("ex")
    exam_dev, coord_dev = gradients.shape
    target_rows = target_features.shape[0]
    n_far, n_y = n_param // 2, n_ex // 2
    width, pair = n_y * BLOCK, 2 * exam_dev
    t_dev = target_rows // n_param
    depth = coord_dev // 2
    bf, f32 = jnp.bfloat16, jnp.float32
    sizes = (n_param, n_ex, exam_dev, coord_dev, target_rows, depth)
    dma = pltpu.SemaphoreType.DMA
    return pl.pallas_call(
        functools.partial(body, sizes),
        out_shape=jax.ShapeDtypeStruct((t_dev, exam_dev), f32),
        in_specs=[
            pl.BlockSpec(memory_space=pltpu.SMEM),
            pl.BlockSpec(memory_space=pl.ANY),
            pl.BlockSpec(memory_space=pl.ANY),
        ],
        out_specs=pl.BlockSpec(memory_space=pltpu.VMEM),
        scratch_shapes=[
            pltpu.VMEM((pair, coord_dev), bf),
            pltpu.VMEM((coord_dev, BLOCK), jnp.int32),
            pltpu.VMEM((n_param, 8, width), jnp.int32),
            pltpu.VMEM((depth, width), bf),
            pltpu.VMEM((depth, width), bf),
            pltpu.VMEM((target_rows, n_ex * BLOCK), bf),
            pltpu.VMEM((pair, width), f32),
            pltpu.VMEM((pair, width), f32),
            pltpu.VMEM((n_far, pair, width), bf),
            pltpu.VMEM((n_far, pair, width), bf),
            pltpu.VMEM((n_far, pair, width), bf),
            pltpu.VMEM((n_far, pair, width), bf),
            pltpu.VMEM((n_y, pair, BLOCK), bf),
            pltpu.VMEM((n_ex * exam_dev, BLOCK), bf),
            pltpu.VMEM((n_ex * exam_dev, BLOCK), bf),
            pltpu.VMEM((exam_dev, n_ex * BLOCK), bf),
            pltpu.VMEM((target_rows, exam_dev), f32),
            pltpu.VMEM((target_rows, exam_dev), bf),
            pltpu.VMEM((n_param - 1, t_dev, exam_dev), bf),
            dma((2,)),
            dma((2, coord_dev // depth)),
            dma((2, n_far)),
            dma((2, n_far)),
            dma((2, n_y)),
            dma((2, n_ex)),
            dma((2, n_param)),
        ],
        compiler_params=pltpu.CompilerParams(
            collective_id=0, has_side_effects=True, vmem_limit_bytes=58 * 2**20
        ),
    )(projection_seed, gradients, target_features)


def kernel_fits(gradients, target_features):
    n_param, n_ex = lax.axis_size("param"), lax.axis_size("ex")
    exam_dev, coord_dev = gradients.shape
    return (
        n_param * n_ex * BLOCK == FEATS
        and n_param % 2 == 0
        and n_param >= 4
        and n_ex % 2 == 0
        and exam_dev % BLOCK == 0
        and coord_dev % 2048 == 0
        and target_features.shape[0] % (16 * n_param) == 0
    )


def partner_2(array, axis, distance):
    return lax.ppermute(array, axis, [(i, i ^ 1 << distance) for i in range(lax.axis_size(axis))])


def hashed(seed_value, row_start, row_count, col_start, col_count, total_coords):
    row_index = (row_start + lax.iota(jnp.int32, row_count)).reshape(row_count, 1)
    col_index = (col_start + lax.iota(jnp.int32, col_count)).reshape(1, col_count)
    mixed = row_index * 73856093 ^ col_index * 19349663 ^ seed_value * 83492791
    mixed = mixed ^ jnp.right_shift(mixed, 13)
    mixed = mixed * 1274126177
    mixed = mixed ^ jnp.right_shift(mixed, 16)
    uniform_value = (mixed & 65535).astype(jnp.float32) * (1.0 / 65536.0)
    return ((2.0 * uniform_value - 1.0) * math.sqrt(3.0 / total_coords)).astype(jnp.bfloat16)


def newton_inverse(fisher):
    width = fisher.shape[1]
    identity = jnp.eye(width, dtype=jnp.float32)
    trace_value = jnp.einsum("bii->b", fisher)
    damped = fisher + (DAMPING * trace_value)[:, None, None] * identity
    total = jnp.einsum("bii->b", damped)
    iterate = identity[None] / total[:, None, None]
    for _ in range(STEPS):
        product = jnp.einsum("bij,bjk->bik", damped, iterate, precision=lax.Precision.HIGHEST)
        iterate = jnp.einsum(
            "bij,bjk->bik", iterate, 2.0 * identity - product, precision=lax.Precision.HIGHEST
        )
    return iterate


def to_targets(partial_scores):
    return lax.all_to_all(partial_scores, "param", split_axis=0, concat_axis=1, tiled=True)


def on_device(gradients, projection_seed, target_features):
    if kernel_fits(gradients, target_features):
        return fused(gradients, projection_seed, target_features)
    seed_value = projection_seed[0]
    my_index = lax.axis_index("param")
    param_count = lax.axis_size("param")
    exam_dev, coord_dev = gradients.shape
    total_coords = coord_dev * param_count
    row_start = my_index * coord_dev
    examples_total = exam_dev * lax.axis_size("ex")
    feats_owned = FEATS // param_count
    piece_width = math.gcd(feats_owned * lax.axis_size("param"), 512)

    def project_piece(col_start):
        matrix = hashed(seed_value, row_start, coord_dev, col_start, piece_width, total_coords)
        return jnp.dot(gradients, matrix, preferred_element_type=jnp.float32).T

    starts = piece_width * lax.iota(jnp.int32, feats_owned * lax.axis_size("param") // piece_width)
    pieces = lax.map(project_piece, starts)
    owned = lax.psum_scatter(
        pieces.reshape(feats_owned * lax.axis_size("param"), exam_dev),
        "param",
        scatter_dimension=0,
        tiled=True,
    ).astype(jnp.bfloat16)
    if feats_owned < BLOCK:
        partner = partner_2(owned, "param", 0)
        is_lower = my_index % 2 == 0
        block_rows = jnp.concatenate(
            [jnp.where(is_lower, owned, partner), jnp.where(is_lower, partner, owned)], 0
        )
    else:
        block_rows = owned
    block_total = block_rows.shape[0] // BLOCK
    blocks = block_rows.reshape(block_total, BLOCK, exam_dev)
    partial_fisher = jnp.einsum("bie,bje->bij", blocks, blocks, preferred_element_type=jnp.float32)
    fisher = lax.psum(partial_fisher, "ex") / examples_total
    inverse_bf = newton_inverse(fisher).astype(jnp.bfloat16)
    conditioned = jnp.einsum("bmj,bme->bje", inverse_bf, blocks, preferred_element_type=jnp.float32)
    conditioned = conditioned.astype(jnp.bfloat16).reshape(block_rows.shape[0], exam_dev)
    if feats_owned < BLOCK:
        conditioned = lax.dynamic_slice_in_dim(
            conditioned, my_index % 2 * feats_owned, feats_owned, 0
        )
    example_rows = lax.all_to_all(conditioned, "param", split_axis=1, concat_axis=0, tiled=True)
    return to_targets(jnp.dot(target_features, example_rows, preferred_element_type=jnp.float32))


def solution(mesh):
    placed = (P("ex", "param"), P(), P())
    return jax.shard_map(
        on_device, mesh=mesh, in_specs=placed, out_specs=P("param", "ex"), check_vma=False
    )
```

```python
import functools
import math

import jax
import jax.numpy as jnp
from jax import lax
from jax.experimental import pallas as pl
from jax.experimental.pallas import tpu as pltpu
from jax.sharding import PartitionSpec as P

FEATS = 4096
BLOCK = 128
STEPS = 10
DAMPING = 0.001
PIECE = 64
MESH = pl.DeviceIdType.MESH


def row_part(start, shape, seed_value):
    row = start + lax.broadcasted_iota(jnp.int32, shape, 0)
    mixed = row * 73856093 ^ seed_value * 83492791
    return mixed ^ jnp.right_shift(mixed, 13) ^ jnp.int32(-(2**31))


def col_part(start, shape):
    col = start + lax.broadcasted_iota(jnp.int32, shape, 1)
    mixed = col * 19349663
    return mixed ^ jnp.right_shift(mixed, 13)


def centred(rows, cols):
    mixed = (rows ^ cols) * 1274126177
    mixed = mixed ^ jnp.left_shift(mixed, 16)
    return jnp.right_shift(mixed, 16).astype(jnp.float32)


def split(values):
    high = values.astype(jnp.bfloat16)
    return high, (values - high.astype(jnp.float32)).astype(jnp.bfloat16)


def body(
    sizes, seed_ref, grad_ref, target_ref, out_ref,
    grads, rows_tab, cols_tab, proj_a, proj_b, targets, acc, mine, xs, xr, zs, zr, ys, feats,
    pre, pre_all, part, part_bf, part_in,
    local_sem, grad_sem, x_sem, z_sem, y_sem, pre_sem, score_sem,
):
    n_param, n_ex, exam_dev, coord_dev, target_rows, depth = sizes
    n_far, n_y = n_param // 2, n_ex // 2
    width = n_y * BLOCK
    p, e = lax.axis_index("param"), lax.axis_index("ex")
    z, x, y, c = p // 2, p % 2, e // 2, e % 2
    pair = 2 * exam_dev
    total_coords = coord_dev * n_param

    def copy(src, dst, sem, slot, pp, ee):
        return pltpu.make_async_remote_copy(
            src_ref=src, dst_ref=dst, send_sem=sem.at[0, slot], recv_sem=sem.at[1, slot],
            device_id=(pp, ee), device_id_type=MESH,
        )

    own_rows = pl.ds(pl.multiple_of(c * exam_dev, exam_dev), exam_dev)
    load_grad = pltpu.make_async_copy(grad_ref, grads.at[own_rows], local_sem.at[0])
    load_grad.start()
    own_cols = pl.ds(pl.multiple_of(p * (n_ex * BLOCK), n_ex * BLOCK), n_ex * BLOCK)
    load_target = pltpu.make_async_copy(target_ref.at[:, own_cols], targets, local_sem.at[1])
    load_target.start()

    barrier = pltpu.get_barrier_semaphore()
    for d in range(1, n_param):
        pl.semaphore_signal(barrier, inc=1, device_id=((p + d) % n_param, e), device_id_type=MESH)
    for d in range(1, n_ex):
        pl.semaphore_signal(barrier, inc=1, device_id=(p, (e + d) % n_ex), device_id_type=MESH)

    order = [("x", s) for s in range(n_far - 1)] + [("m", s) for s in range(n_far - 1)]
    order += [("x", n_far - 1), ("m", n_far - 1)]

    def far(s):
        return (z + 1 + s) % n_far

    def half(t, start, size):
        return pl.ds(pl.multiple_of(t * depth + start, size), size)

    def make(proj, t, i, start, size):
        for k in range(start, start + size, PIECE):
            rows = rows_tab[half(t, k, PIECE), :].reshape(PIECE // 8, 8, BLOCK)
            for w in range(0, width, BLOCK):
                values = centred(rows, cols_tab[i, :, w : w + BLOCK][None])
                values = values.reshape(PIECE, BLOCK).astype(jnp.bfloat16)
                proj[k : k + PIECE, w : w + BLOCK] = values

    def block(now, t, later=None, later_t=None, later_i=None):
        if later is not None:
            make(later, later_t, later_i, 0, depth)
        product = jnp.dot(grads[:, half(t, 0, depth)], now[...], preferred_element_type=jnp.float32)
        if t == 0:
            acc[...] = product
        else:
            acc[...] += product

    def swap(t):
        here = pl.ds(t * depth, depth)
        return copy(grad_ref.at[:, here], grads.at[own_rows, here], grad_sem, t, p, e + 1 - 2 * c)

    pl.semaphore_wait(barrier, n_param - 1 + n_ex - 1)
    for t in range(2):
        swap(t).start()
    seed_value = seed_ref[0]
    rows_tab[...] = row_part(p * coord_dev, rows_tab.shape, seed_value)
    for i, (kind, s) in enumerate(order):
        to = far(s) * 2 + (1 - x if kind == "x" else x)
        cols_tab[i] = col_part(to * (n_ex * BLOCK) + c * width, (8, width))

    make(proj_a, 0, 0, 0, depth)
    load_grad.wait()

    def x_copy(s):
        return copy(xs.at[s], xr.at[s], x_sem, s, p + 1 - 2 * x, e)

    def z_copy(s):
        return copy(zs.at[s], zr.at[s], z_sem, s, far(s) * 2 + x, e)

    def swapped(t, i):
        @pl.when(i == 0)
        def _():
            swap(t).wait()

    def chunk(i, carry):
        swapped(0, i)
        block(proj_a, 0, proj_b, 1, i)
        swapped(1, i)
        block(proj_b, 1, proj_a, 0, i + 1)
        to_pair = jnp.logical_or(i < n_far - 1, i == n_param - 2)

        @pl.when(to_pair)
        def _():
            s = jnp.minimum(i, n_far - 1)
            xs[s] = acc[...].astype(jnp.bfloat16)
            x_copy(s).start()

        @pl.when(jnp.logical_not(to_pair))
        def _():
            s = i - (n_far - 1)
            x_copy(s).wait_recv()
            zs[s] = (acc[...] + xr[s].astype(jnp.float32)).astype(jnp.bfloat16)
            z_copy(s).start()

        return carry

    lax.fori_loop(0, n_param - 1, chunk, 0)
    block(proj_a, 0, proj_b, 1, n_param - 1)
    block(proj_b, 1)
    x_copy(n_far - 1).wait_recv()
    total = acc[...] + xr[n_far - 1].astype(jnp.float32)
    for s in range(n_far - 1):
        z_copy(s).wait_recv()
        total = total + zr[s].astype(jnp.float32)
    total = (total * (math.sqrt(3.0 / total_coords) / 32768.0)).astype(jnp.bfloat16)
    for k in range(n_y):
        ys[k] = total[:, k * BLOCK : (k + 1) * BLOCK]
    my_pair = pl.ds(pl.multiple_of(y * pair, pair), pair)
    y_copies = []
    for d in range(1, n_y):
        there = (y + d) % n_y
        copy_y = copy(ys.at[there], feats.at[my_pair], y_sem, d - 1, p, there * 2 + c)
        copy_y.start()
        y_copies.append(copy_y)
    feats[my_pair, :] = ys[y]
    for copy_y in y_copies:
        copy_y.wait_recv()

    fisher = lax.dot_general(
        feats[...], feats[...], (((0,), (0,)), ((), ())), preferred_element_type=jnp.float32
    ) / (n_ex * exam_dev)
    eye = (
        lax.broadcasted_iota(jnp.int32, (BLOCK, BLOCK), 0)
        == lax.broadcasted_iota(jnp.int32, (BLOCK, BLOCK), 1)
    ).astype(jnp.float32)

    def trace(square):
        return jnp.sum(jnp.sum(square * eye, axis=0, keepdims=True), axis=1, keepdims=True)

    damped = fisher + (DAMPING * trace(fisher)) * eye
    inverse = eye / trace(damped)
    gap = eye - damped / trace(damped)
    for step_index in range(STEPS):
        last = step_index == STEPS - 1
        high, low = split(inverse if last else jnp.concatenate([inverse, gap], 0))
        gap_high, gap_low = split(gap) if last else (high[BLOCK:], low[BLOCK:])
        both = jnp.dot(
            jnp.concatenate([high, low, high], 1),
            jnp.concatenate([gap_high, gap_high, gap_low], 0),
            preferred_element_type=jnp.float32,
        )
        inverse = inverse + both[:BLOCK]
        gap = both[BLOCK:]
    pre[...] = jnp.dot(
        feats[...], inverse.astype(jnp.bfloat16), preferred_element_type=jnp.float32
    ).astype(jnp.bfloat16)

    slot = pl.ds(pl.multiple_of((c * n_y + y) * BLOCK, BLOCK), BLOCK)
    pre_copies = []
    for d in range(1, n_ex):
        there = (e + d) % n_ex
        src = pre.at[pl.ds(pl.multiple_of(there * exam_dev, exam_dev), exam_dev)]
        copy_p = copy(src, pre_all.at[:, slot], pre_sem, d - 1, p, there)
        copy_p.start()
        pre_copies.append(copy_p)
    pre_all[:, slot] = pre[pl.ds(pl.multiple_of(e * exam_dev, exam_dev), exam_dev), :]
    load_target.wait()
    for copy_p in pre_copies:
        copy_p.wait_recv()

    part[...] = lax.dot_general(
        targets[...], pre_all[...], (((1,), (1,)), ((), ())), preferred_element_type=jnp.float32
    )
    part_bf[...] = part[...].astype(jnp.bfloat16)
    t_dev = target_rows // n_param
    score_copies = []
    for d in range(1, n_param):
        there = (p + d) % n_param
        src = part_bf.at[pl.ds(pl.multiple_of(there * t_dev, t_dev), t_dev)]
        copy_s = copy(src, part_in.at[d - 1], score_sem, d - 1, there, e)
        copy_s.start()
        score_copies.append(copy_s)
    result = part[pl.ds(pl.multiple_of(p * t_dev, t_dev), t_dev), :]
    for d in range(1, n_param):
        score_copies[d - 1].wait_recv()
        result = result + part_in[d - 1].astype(jnp.float32)
    out_ref[...] = result
    sent = [x_copy(s) for s in range(n_far)] + [z_copy(s) for s in range(n_far - 1)]
    for one in sent + y_copies + pre_copies + score_copies:
        one.wait_send()


def fused(gradients, projection_seed, target_features):
    n_param, n_ex = lax.axis_size("param"), lax.axis_size("ex")
    exam_dev, coord_dev = gradients.shape
    target_rows = target_features.shape[0]
    n_far, n_y = n_param // 2, n_ex // 2
    width, pair = n_y * BLOCK, 2 * exam_dev
    t_dev = target_rows // n_param
    depth = coord_dev // 2
    bf, f32 = jnp.bfloat16, jnp.float32
    sizes = (n_param, n_ex, exam_dev, coord_dev, target_rows, depth)
    dma = pltpu.SemaphoreType.DMA
    return pl.pallas_call(
        functools.partial(body, sizes),
        out_shape=jax.ShapeDtypeStruct((t_dev, exam_dev), f32),
        in_specs=[
            pl.BlockSpec(memory_space=pltpu.SMEM),
            pl.BlockSpec(memory_space=pl.ANY),
            pl.BlockSpec(memory_space=pl.ANY),
        ],
        out_specs=pl.BlockSpec(memory_space=pltpu.VMEM),
        scratch_shapes=[
            pltpu.VMEM((pair, coord_dev), bf),
            pltpu.VMEM((coord_dev, BLOCK), jnp.int32),
            pltpu.VMEM((n_param, 8, width), jnp.int32),
            pltpu.VMEM((depth, width), bf),
            pltpu.VMEM((depth, width), bf),
            pltpu.VMEM((target_rows, n_ex * BLOCK), bf),
            pltpu.VMEM((pair, width), f32),
            pltpu.VMEM((pair, width), f32),
            pltpu.VMEM((n_far, pair, width), bf),
            pltpu.VMEM((n_far, pair, width), bf),
            pltpu.VMEM((n_far, pair, width), bf),
            pltpu.VMEM((n_far, pair, width), bf),
            pltpu.VMEM((n_y, pair, BLOCK), bf),
            pltpu.VMEM((n_ex * exam_dev, BLOCK), bf),
            pltpu.VMEM((n_ex * exam_dev, BLOCK), bf),
            pltpu.VMEM((exam_dev, n_ex * BLOCK), bf),
            pltpu.VMEM((target_rows, exam_dev), f32),
            pltpu.VMEM((target_rows, exam_dev), bf),
            pltpu.VMEM((n_param - 1, t_dev, exam_dev), bf),
            dma((2,)),
            dma((2, coord_dev // depth)),
            dma((2, n_far)),
            dma((2, n_far)),
            dma((2, n_y)),
            dma((2, n_ex)),
            dma((2, n_param)),
        ],
        compiler_params=pltpu.CompilerParams(
            collective_id=0, has_side_effects=True, vmem_limit_bytes=58 * 2**20
        ),
    )(projection_seed, gradients, target_features)


def kernel_fits(gradients, target_features):
    n_param, n_ex = lax.axis_size("param"), lax.axis_size("ex")
    exam_dev, coord_dev = gradients.shape
    return (
        n_param * n_ex * BLOCK == FEATS
        and n_param % 2 == 0
        and n_param >= 4
        and n_ex % 2 == 0
        and exam_dev % BLOCK == 0
        and coord_dev % 2048 == 0
        and target_features.shape[0] % (16 * n_param) == 0
    )


def partner_2(array, axis, distance):
    return lax.ppermute(array, axis, [(i, i ^ 1 << distance) for i in range(lax.axis_size(axis))])


def hashed(seed_value, row_start, row_count, col_start, col_count, total_coords):
    row_index = (row_start + lax.iota(jnp.int32, row_count)).reshape(row_count, 1)
    col_index = (col_start + lax.iota(jnp.int32, col_count)).reshape(1, col_count)
    mixed = row_index * 73856093 ^ col_index * 19349663 ^ seed_value * 83492791
    mixed = mixed ^ jnp.right_shift(mixed, 13)
    mixed = mixed * 1274126177
    mixed = mixed ^ jnp.right_shift(mixed, 16)
    uniform_value = (mixed & 65535).astype(jnp.float32) * (1.0 / 65536.0)
    return ((2.0 * uniform_value - 1.0) * math.sqrt(3.0 / total_coords)).astype(jnp.bfloat16)


def newton_inverse(fisher):
    width = fisher.shape[1]
    identity = jnp.eye(width, dtype=jnp.float32)
    trace_value = jnp.einsum("bii->b", fisher)
    damped = fisher + (DAMPING * trace_value)[:, None, None] * identity
    total = jnp.einsum("bii->b", damped)
    iterate = identity[None] / total[:, None, None]
    for _ in range(STEPS):
        product = jnp.einsum("bij,bjk->bik", damped, iterate, precision=lax.Precision.HIGHEST)
        iterate = jnp.einsum(
            "bij,bjk->bik", iterate, 2.0 * identity - product, precision=lax.Precision.HIGHEST
        )
    return iterate


def to_targets(partial_scores):
    return lax.all_to_all(partial_scores, "param", split_axis=0, concat_axis=1, tiled=True)


def on_device(gradients, projection_seed, target_features):
    if kernel_fits(gradients, target_features):
        return fused(gradients, projection_seed, target_features)
    seed_value = projection_seed[0]
    my_index = lax.axis_index("param")
    param_count = lax.axis_size("param")
    exam_dev, coord_dev = gradients.shape
    total_coords = coord_dev * param_count
    row_start = my_index * coord_dev
    examples_total = exam_dev * lax.axis_size("ex")
    feats_owned = FEATS // param_count
    piece_width = math.gcd(feats_owned * lax.axis_size("param"), 512)

    def project_piece(col_start):
        matrix = hashed(seed_value, row_start, coord_dev, col_start, piece_width, total_coords)
        return jnp.dot(gradients, matrix, preferred_element_type=jnp.float32).T

    starts = piece_width * lax.iota(jnp.int32, feats_owned * lax.axis_size("param") // piece_width)
    pieces = lax.map(project_piece, starts)
    owned = lax.psum_scatter(
        pieces.reshape(feats_owned * lax.axis_size("param"), exam_dev),
        "param",
        scatter_dimension=0,
        tiled=True,
    ).astype(jnp.bfloat16)
    if feats_owned < BLOCK:
        partner = partner_2(owned, "param", 0)
        is_lower = my_index % 2 == 0
        block_rows = jnp.concatenate(
            [jnp.where(is_lower, owned, partner), jnp.where(is_lower, partner, owned)], 0
        )
    else:
        block_rows = owned
    block_total = block_rows.shape[0] // BLOCK
    blocks = block_rows.reshape(block_total, BLOCK, exam_dev)
    partial_fisher = jnp.einsum("bie,bje->bij", blocks, blocks, preferred_element_type=jnp.float32)
    fisher = lax.psum(partial_fisher, "ex") / examples_total
    inverse_bf = newton_inverse(fisher).astype(jnp.bfloat16)
    conditioned = jnp.einsum("bmj,bme->bje", inverse_bf, blocks, preferred_element_type=jnp.float32)
    conditioned = conditioned.astype(jnp.bfloat16).reshape(block_rows.shape[0], exam_dev)
    if feats_owned < BLOCK:
        conditioned = lax.dynamic_slice_in_dim(
            conditioned, my_index % 2 * feats_owned, feats_owned, 0
        )
    example_rows = lax.all_to_all(conditioned, "param", split_axis=1, concat_axis=0, tiled=True)
    return to_targets(jnp.dot(target_features, example_rows, preferred_element_type=jnp.float32))


def solution(mesh):
    placed = (P("ex", "param"), P(), P())
    return jax.shard_map(
        on_device, mesh=mesh, in_specs=placed, out_specs=P("param", "ex"), check_vma=False
    )
```

```python
import functools
import math

import jax
import jax.numpy as jnp
from jax import lax
from jax.experimental import pallas as pl
from jax.experimental.pallas import tpu as pltpu
from jax.sharding import PartitionSpec as P

FEATS = 4096
BLOCK = 128
STEPS = 10
DAMPING = 0.001
PIECE = 64
MESH = pl.DeviceIdType.MESH


def row_part(start, shape, seed_value):
    row = start + lax.broadcasted_iota(jnp.int32, shape, 0)
    mixed = row * 73856093 ^ seed_value * 83492791
    return mixed ^ jnp.right_shift(mixed, 13) ^ jnp.int32(-(2**31))


def col_part(start, shape):
    col = start + lax.broadcasted_iota(jnp.int32, shape, 1)
    mixed = col * 19349663
    return mixed ^ jnp.right_shift(mixed, 13)


def centred(rows, cols):
    mixed = (rows ^ cols) * 1274126177
    mixed = mixed ^ jnp.left_shift(mixed, 16)
    return jnp.right_shift(mixed, 16).astype(jnp.float32)


def split(values):
    high = values.astype(jnp.bfloat16)
    return high, (values - high.astype(jnp.float32)).astype(jnp.bfloat16)


def body(
    sizes, seed_ref, grad_ref, target_ref, out_ref,
    grads, rows_tab, cols_tab, proj_a, proj_b, targets, acc, mine, xs, xr, zs, zr, ys, feats,
    pre, pre_all, part, part_bf, part_in,
    local_sem, grad_sem, x_sem, z_sem, y_sem, pre_sem, score_sem,
):
    n_param, n_ex, exam_dev, coord_dev, target_rows, depth = sizes
    n_far, n_y = n_param // 2, n_ex // 2
    width = n_y * BLOCK
    p, e = lax.axis_index("param"), lax.axis_index("ex")
    z, x, y, c = p // 2, p % 2, e // 2, e % 2
    pair = 2 * exam_dev
    total_coords = coord_dev * n_param

    def copy(src, dst, sem, slot, pp, ee):
        return pltpu.make_async_remote_copy(
            src_ref=src, dst_ref=dst, send_sem=sem.at[0, slot], recv_sem=sem.at[1, slot],
            device_id=(pp, ee), device_id_type=MESH,
        )

    own_rows = pl.ds(pl.multiple_of(c * exam_dev, exam_dev), exam_dev)
    load_grad = pltpu.make_async_copy(grad_ref, grads.at[own_rows], local_sem.at[0])
    load_grad.start()
    own_cols = pl.ds(pl.multiple_of(p * (n_ex * BLOCK), n_ex * BLOCK), n_ex * BLOCK)
    load_target = pltpu.make_async_copy(target_ref.at[:, own_cols], targets, local_sem.at[1])
    load_target.start()

    barrier = pltpu.get_barrier_semaphore()
    for d in range(1, n_param):
        pl.semaphore_signal(barrier, inc=1, device_id=((p + d) % n_param, e), device_id_type=MESH)
    for d in range(1, n_ex):
        pl.semaphore_signal(barrier, inc=1, device_id=(p, (e + d) % n_ex), device_id_type=MESH)

    tiles = coord_dev // depth
    projs = (proj_a, proj_b)

    order = [("x", s) for s in range(n_far - 1)] + [("m", s) for s in range(n_far - 1)]
    order += [("x", n_far - 1), ("m", n_far - 1)]

    def far(s):
        return (z + 1 + s) % n_far

    def make(proj, t, i):
        start = pl.multiple_of(t * depth, depth)
        for k in range(0, depth, PIECE):
            here = pl.ds(pl.multiple_of(start + k, PIECE), PIECE)
            rows = rows_tab[here, :].reshape(PIECE // 8, 8, BLOCK)
            for w in range(0, width, BLOCK):
                values = centred(rows, cols_tab[i, :, w : w + BLOCK][None])
                proj[here, w : w + BLOCK] = values.reshape(PIECE, BLOCK).astype(jnp.bfloat16)

    def use(proj, t):
        here = pl.ds(pl.multiple_of(t * depth, depth), depth)
        acc[...] += jnp.dot(grads[:, here], proj[here, :], preferred_element_type=jnp.float32)

    def swap(t):
        here = pl.ds(pl.multiple_of(t * depth, depth), depth)
        return copy(grad_ref.at[:, here], grads.at[own_rows, here], grad_sem, t, p, e + 1 - 2 * c)

    def first(t, carry):
        swap(t).start()
        return carry

    def ahead(t, carry):
        make(projs[0], t, 0)
        make(projs[1], t, 1)
        return carry

    pl.semaphore_wait(barrier, n_param - 1 + n_ex - 1)
    lax.fori_loop(0, tiles, first, 0)
    seed_value = seed_ref[0]
    rows_tab[...] = row_part(p * coord_dev, rows_tab.shape, seed_value)
    for i, (kind, s) in enumerate(order):
        to = far(s) * 2 + (1 - x if kind == "x" else x)
        cols_tab[i] = col_part(to * (n_ex * BLOCK) + c * width, (8, width))

    lax.fori_loop(0, tiles, ahead, 0)
    load_grad.wait()

    x_copies, z_copies = [], []
    for i, (kind, s) in enumerate(order):
        acc[...] = jnp.zeros_like(acc)

        def step(t, carry):
            if i == 0:
                swap(t).wait()
            if 0 < i < len(order) - 1:
                make(projs[(i + 1) % 2], t, i + 1)
            use(projs[i % 2], t)
            return carry

        lax.fori_loop(0, tiles, step, 0)
        if kind == "x":
            xs[s] = acc[...].astype(jnp.bfloat16)
            copy_x = copy(xs.at[s], xr.at[s], x_sem, s, p + 1 - 2 * x, e)
            copy_x.start()
            x_copies.append(copy_x)
        else:
            x_copies[s].wait_recv()
            both = acc[...] + xr[s].astype(jnp.float32)
            if s < n_far - 1:
                zs[s] = both.astype(jnp.bfloat16)
                copy_z = copy(zs.at[s], zr.at[s], z_sem, s, far(s) * 2 + x, e)
                copy_z.start()
                z_copies.append(copy_z)
            else:
                mine[...] = both

    total = mine[...]
    for s in range(n_far - 1):
        z_copies[s].wait_recv()
        total = total + zr[s].astype(jnp.float32)
    total = (total * (math.sqrt(3.0 / total_coords) / 32768.0)).astype(jnp.bfloat16)
    for k in range(n_y):
        ys[k] = total[:, k * BLOCK : (k + 1) * BLOCK]
    my_pair = pl.ds(pl.multiple_of(y * pair, pair), pair)
    y_copies = []
    for d in range(1, n_y):
        there = (y + d) % n_y
        copy_y = copy(ys.at[there], feats.at[my_pair], y_sem, d - 1, p, there * 2 + c)
        copy_y.start()
        y_copies.append(copy_y)
    feats[my_pair, :] = ys[y]
    for copy_y in y_copies:
        copy_y.wait_recv()

    fisher = lax.dot_general(
        feats[...], feats[...], (((0,), (0,)), ((), ())), preferred_element_type=jnp.float32
    ) / (n_ex * exam_dev)
    eye = (
        lax.broadcasted_iota(jnp.int32, (BLOCK, BLOCK), 0)
        == lax.broadcasted_iota(jnp.int32, (BLOCK, BLOCK), 1)
    ).astype(jnp.float32)

    def trace(square):
        return jnp.sum(jnp.sum(square * eye, axis=0, keepdims=True), axis=1, keepdims=True)

    damped = fisher + (DAMPING * trace(fisher)) * eye
    inverse = eye / trace(damped)
    gap = eye - damped / trace(damped)
    for step_index in range(STEPS):
        last = step_index == STEPS - 1
        high, low = split(inverse if last else jnp.concatenate([inverse, gap], 0))
        gap_high, gap_low = split(gap) if last else (high[BLOCK:], low[BLOCK:])
        both = jnp.dot(
            jnp.concatenate([high, low, high], 1),
            jnp.concatenate([gap_high, gap_high, gap_low], 0),
            preferred_element_type=jnp.float32,
        )
        inverse = inverse + both[:BLOCK]
        gap = both[BLOCK:]
    pre[...] = jnp.dot(
        feats[...], inverse.astype(jnp.bfloat16), preferred_element_type=jnp.float32
    ).astype(jnp.bfloat16)

    slot = pl.ds(pl.multiple_of((c * n_y + y) * BLOCK, BLOCK), BLOCK)
    pre_copies = []
    for d in range(1, n_ex):
        there = (e + d) % n_ex
        src = pre.at[pl.ds(pl.multiple_of(there * exam_dev, exam_dev), exam_dev)]
        copy_p = copy(src, pre_all.at[:, slot], pre_sem, d - 1, p, there)
        copy_p.start()
        pre_copies.append(copy_p)
    pre_all[:, slot] = pre[pl.ds(pl.multiple_of(e * exam_dev, exam_dev), exam_dev), :]
    load_target.wait()
    for copy_p in pre_copies:
        copy_p.wait_recv()

    part[...] = lax.dot_general(
        targets[...], pre_all[...], (((1,), (1,)), ((), ())), preferred_element_type=jnp.float32
    )
    part_bf[...] = part[...].astype(jnp.bfloat16)
    t_dev = target_rows // n_param
    score_copies = []
    for d in range(1, n_param):
        there = (p + d) % n_param
        src = part_bf.at[pl.ds(pl.multiple_of(there * t_dev, t_dev), t_dev)]
        copy_s = copy(src, part_in.at[d - 1], score_sem, d - 1, there, e)
        copy_s.start()
        score_copies.append(copy_s)
    result = part[pl.ds(pl.multiple_of(p * t_dev, t_dev), t_dev), :]
    for d in range(1, n_param):
        score_copies[d - 1].wait_recv()
        result = result + part_in[d - 1].astype(jnp.float32)
    out_ref[...] = result
    for group in (x_copies, z_copies, y_copies, pre_copies, score_copies):
        for one in group:
            one.wait_send()


def fused(gradients, projection_seed, target_features):
    n_param, n_ex = lax.axis_size("param"), lax.axis_size("ex")
    exam_dev, coord_dev = gradients.shape
    target_rows = target_features.shape[0]
    n_far, n_y = n_param // 2, n_ex // 2
    width, pair = n_y * BLOCK, 2 * exam_dev
    t_dev = target_rows // n_param
    depth = math.gcd(coord_dev, 4096)
    bf, f32 = jnp.bfloat16, jnp.float32
    sizes = (n_param, n_ex, exam_dev, coord_dev, target_rows, depth)
    dma = pltpu.SemaphoreType.DMA
    return pl.pallas_call(
        functools.partial(body, sizes),
        out_shape=jax.ShapeDtypeStruct((t_dev, exam_dev), f32),
        in_specs=[
            pl.BlockSpec(memory_space=pltpu.SMEM),
            pl.BlockSpec(memory_space=pl.ANY),
            pl.BlockSpec(memory_space=pl.ANY),
        ],
        out_specs=pl.BlockSpec(memory_space=pltpu.VMEM),
        scratch_shapes=[
            pltpu.VMEM((pair, coord_dev), bf),
            pltpu.VMEM((coord_dev, BLOCK), jnp.int32),
            pltpu.VMEM((n_param, 8, width), jnp.int32),
            pltpu.VMEM((coord_dev, width), bf),
            pltpu.VMEM((coord_dev, width), bf),
            pltpu.VMEM((target_rows, n_ex * BLOCK), bf),
            pltpu.VMEM((pair, width), f32),
            pltpu.VMEM((pair, width), f32),
            pltpu.VMEM((n_far, pair, width), bf),
            pltpu.VMEM((n_far, pair, width), bf),
            pltpu.VMEM((n_far, pair, width), bf),
            pltpu.VMEM((n_far, pair, width), bf),
            pltpu.VMEM((n_y, pair, BLOCK), bf),
            pltpu.VMEM((n_ex * exam_dev, BLOCK), bf),
            pltpu.VMEM((n_ex * exam_dev, BLOCK), bf),
            pltpu.VMEM((exam_dev, n_ex * BLOCK), bf),
            pltpu.VMEM((target_rows, exam_dev), f32),
            pltpu.VMEM((target_rows, exam_dev), bf),
            pltpu.VMEM((n_param - 1, t_dev, exam_dev), bf),
            dma((2,)),
            dma((2, coord_dev // depth)),
            dma((2, n_far)),
            dma((2, n_far)),
            dma((2, n_y)),
            dma((2, n_ex)),
            dma((2, n_param)),
        ],
        compiler_params=pltpu.CompilerParams(
            collective_id=0, has_side_effects=True, vmem_limit_bytes=58 * 2**20
        ),
    )(projection_seed, gradients, target_features)


def kernel_fits(gradients, target_features):
    n_param, n_ex = lax.axis_size("param"), lax.axis_size("ex")
    exam_dev, coord_dev = gradients.shape
    return (
        n_param * n_ex * BLOCK == FEATS
        and n_param % 2 == 0
        and n_ex % 2 == 0
        and exam_dev % BLOCK == 0
        and coord_dev % 2048 == 0
        and target_features.shape[0] % (16 * n_param) == 0
    )


def partner_2(array, axis, distance):
    return lax.ppermute(array, axis, [(i, i ^ 1 << distance) for i in range(lax.axis_size(axis))])


def hashed(seed_value, row_start, row_count, col_start, col_count, total_coords):
    row_index = (row_start + lax.iota(jnp.int32, row_count)).reshape(row_count, 1)
    col_index = (col_start + lax.iota(jnp.int32, col_count)).reshape(1, col_count)
    mixed = row_index * 73856093 ^ col_index * 19349663 ^ seed_value * 83492791
    mixed = mixed ^ jnp.right_shift(mixed, 13)
    mixed = mixed * 1274126177
    mixed = mixed ^ jnp.right_shift(mixed, 16)
    uniform_value = (mixed & 65535).astype(jnp.float32) * (1.0 / 65536.0)
    return ((2.0 * uniform_value - 1.0) * math.sqrt(3.0 / total_coords)).astype(jnp.bfloat16)


def newton_inverse(fisher):
    width = fisher.shape[1]
    identity = jnp.eye(width, dtype=jnp.float32)
    trace_value = jnp.einsum("bii->b", fisher)
    damped = fisher + (DAMPING * trace_value)[:, None, None] * identity
    total = jnp.einsum("bii->b", damped)
    iterate = identity[None] / total[:, None, None]
    for _ in range(STEPS):
        product = jnp.einsum("bij,bjk->bik", damped, iterate, precision=lax.Precision.HIGHEST)
        iterate = jnp.einsum(
            "bij,bjk->bik", iterate, 2.0 * identity - product, precision=lax.Precision.HIGHEST
        )
    return iterate


def to_targets(partial_scores):
    return lax.all_to_all(partial_scores, "param", split_axis=0, concat_axis=1, tiled=True)


def on_device(gradients, projection_seed, target_features):
    if kernel_fits(gradients, target_features):
        return fused(gradients, projection_seed, target_features)
    seed_value = projection_seed[0]
    my_index = lax.axis_index("param")
    param_count = lax.axis_size("param")
    exam_dev, coord_dev = gradients.shape
    total_coords = coord_dev * param_count
    row_start = my_index * coord_dev
    examples_total = exam_dev * lax.axis_size("ex")
    feats_owned = FEATS // param_count
    piece_width = math.gcd(feats_owned * lax.axis_size("param"), 512)

    def project_piece(col_start):
        matrix = hashed(seed_value, row_start, coord_dev, col_start, piece_width, total_coords)
        return jnp.dot(gradients, matrix, preferred_element_type=jnp.float32).T

    starts = piece_width * lax.iota(jnp.int32, feats_owned * lax.axis_size("param") // piece_width)
    pieces = lax.map(project_piece, starts)
    owned = lax.psum_scatter(
        pieces.reshape(feats_owned * lax.axis_size("param"), exam_dev),
        "param",
        scatter_dimension=0,
        tiled=True,
    ).astype(jnp.bfloat16)
    if feats_owned < BLOCK:
        partner = partner_2(owned, "param", 0)
        is_lower = my_index % 2 == 0
        block_rows = jnp.concatenate(
            [jnp.where(is_lower, owned, partner), jnp.where(is_lower, partner, owned)], 0
        )
    else:
        block_rows = owned
    block_total = block_rows.shape[0] // BLOCK
    blocks = block_rows.reshape(block_total, BLOCK, exam_dev)
    partial_fisher = jnp.einsum("bie,bje->bij", blocks, blocks, preferred_element_type=jnp.float32)
    fisher = lax.psum(partial_fisher, "ex") / examples_total
    inverse_bf = newton_inverse(fisher).astype(jnp.bfloat16)
    conditioned = jnp.einsum("bmj,bme->bje", inverse_bf, blocks, preferred_element_type=jnp.float32)
    conditioned = conditioned.astype(jnp.bfloat16).reshape(block_rows.shape[0], exam_dev)
    if feats_owned < BLOCK:
        conditioned = lax.dynamic_slice_in_dim(
            conditioned, my_index % 2 * feats_owned, feats_owned, 0
        )
    example_rows = lax.all_to_all(conditioned, "param", split_axis=1, concat_axis=0, tiled=True)
    return to_targets(jnp.dot(target_features, example_rows, preferred_element_type=jnp.float32))


def solution(mesh):
    placed = (P("ex", "param"), P(), P())
    return jax.shard_map(
        on_device, mesh=mesh, in_specs=placed, out_specs=P("param", "ex"), check_vma=False
    )
```
